128 devices in a mesh: index: 16 (over x, z), reader: 8 (over y, core).
Axes of the slice: x: 4, y: 4, z: 4, core: 2. Of those that a mesh axis runs over, the one named last changes fastest.
Arguments:
- question_emb: bfloat16 [128, 768], P(('index', 'reader')), may hold values from -6 to 6
- probes: int32 [128, 32], P(('index', 'reader')), may hold values from 0 to 511, all different within a row
- codes: bfloat16 [512, 128, 768], P('index'), may hold values from -0.21875 to 0.21875
- code_scale: float32 [512, 128], P('index'), may hold values from 0.25 to 4
- question_state: bfloat16 [128, 2048], P(('index', 'reader')), may hold values from -6 to 6
- top_passages: int32 [128, 20], P(('index', 'reader')), may hold values from 0 to 4095, as said below
- soft_weight: float32 [128, 20], P(('index', 'reader')), may hold values from 0.02 to 0.5
- passage_home: int32 [4096], replicated, may hold values from 0 to 4095, as said below
- passage_states: bfloat16 [4096, 8, 2048], P('index'), may hold values from -6 to 6
- norm_gain: float32 [2048], replicated, may hold values from 0.25 to 1.75
- w_gate: bfloat16 [2048, 4096], P(None, 'index'), may hold values from -0.125 to 0.125
- w_up: bfloat16 [2048, 4096], P(None, 'index'), may hold values from -0.125 to 0.125
- w_out: bfloat16 [4096, 2048], P('index'), may hold values from -0.09375 to 0.09375
- cotangent: bfloat16 [128, 20, 8, 2048], P(('index', 'reader')), may hold values from -3 to 3
Outputs:
- probe_scores: float32 [128, 32, 128], P(('index', 'reader'))
- grad_out: float32 [4096, 2048], P('index', 'reader')
- grad_gain: float32 [2048], P(('index', 'reader'))
The draws below stay inside these ranges and needn't reach their ends.
Inputs may be any that keep to these rules, and one draw needn't show every extreme that they name: `probes`: each question names 32 different clusters; every cluster is named by some question. A permutation: passage p's state is row passage_home[p] of passage_states, held by index shard passage_home[p] // 256. `top_passages`: each question names 20 different passages, at most 3 of them held by one index shard. For the questions of the devices with one reader index, some index shard holds exactly 3 passages of each of them.
All inputs are finite; a program needn't handle non-finite values.
Results may differ from the reference program's by a relative error of at most 0.022.
Values may be sent and summed in bfloat16 or wider, within the bound.
No kernel may reach another device: no remote copies, remote signals or barrier semaphores. Data moves between devices by JAX's collectives and lax.ppermute only.
A program may use at most 256 MiB of HBM per device.

```python
import math
import jax
import jax.numpy as jnp
from jax import lax

D = 2048
FW = 4096
E = 768
CSIZE = 128
NPROBE = 32
TOPK = 20
CAP = 3
LP = 8
QD = 1
PASS_DEV = 256
QUESTIONS = 128
CLUSTERS = 512
PASSAGES = 4096
N_INDEX = 16
N_READER = 8


def request_plan(key):
    home = jax.random.permutation(jax.random.fold_in(key, 11), PASSAGES).astype(jnp.int32)
    inverse = jnp.argsort(home, stable=True).astype(jnp.int32)
    question = jnp.arange(QUESTIONS, dtype=jnp.int32)
    group = question // QD % N_READER
    hot_owner = jax.random.randint(jax.random.fold_in(key, 12), (N_READER,), 0, N_INDEX)[group]
    others = N_INDEX - 1
    popular = jax.random.randint(jax.random.fold_in(key, 13), (N_INDEX,), 0, 4)
    other_slot = jnp.arange(others, dtype=jnp.int32)[None, :]
    owner_other = other_slot + (other_slot >= hot_owner[:, None]).astype(jnp.int32)
    raw_score = jax.random.randint(jax.random.fold_in(key, 14), (QUESTIONS, others, CAP), 0, 2 ** 15)
    bias = popular[owner_other] * 2 ** 14
    count = others * CAP
    ordinal = jnp.arange(count, dtype=jnp.int32).reshape(others, CAP)
    score = ((raw_score + bias[:, :, None]) * count + ordinal[None]).reshape(QUESTIONS, count)
    _, picked = lax.top_k(score, TOPK - CAP)
    picked_owner = jnp.take_along_axis(owner_other, picked // CAP, axis=1)
    picked_copy = picked % CAP
    owners = jnp.concatenate([jnp.broadcast_to(hot_owner[:, None], (QUESTIONS, CAP)), picked_owner], axis=1)
    copies = jnp.concatenate([jnp.broadcast_to(jnp.arange(CAP, dtype=jnp.int32)[None, :], (QUESTIONS, CAP)), picked_copy], axis=1)
    stride = PASS_DEV // CAP
    base = jax.random.randint(jax.random.fold_in(key, 15), (QUESTIONS, N_INDEX), 0, stride)
    local_row = jnp.take_along_axis(base, owners, axis=1) + copies * stride
    passage_ids = inverse[owners * PASS_DEV + local_row]
    order_score = jax.random.randint(jax.random.fold_in(key, 16), (QUESTIONS, TOPK), 0, 2 ** 15) * TOPK + jnp.arange(TOPK, dtype=jnp.int32)[None, :]
    order = jnp.argsort(order_score, axis=1, stable=True)
    passage_ids = jnp.take_along_axis(passage_ids, order, axis=1)
    return (home, passage_ids.astype(jnp.int32))


def draw_passage_home(key, part):
    home, passage_ids = request_plan(key)
    return home


def draw_top_passages(key, part):
    home, passage_ids = request_plan(key)
    return passage_ids


def with_spikes(values, stream_key, source, target, parts, factor):
    def block_of(dim):
        return (jnp.arange(values.shape[dim]) // (values.shape[dim] // parts)).reshape((-1,) + (1,) * (values.ndim - 1 - dim))

    near = jax.random.permutation(stream_key, parts)[block_of(target)]
    second = (block_of(target) + parts // 2) % parts
    return jnp.where((block_of(source) == near) | (block_of(source) == second), factor * values, values)


def levels(rng, shape, pieces, low, top_value):
    gain = 1.0
    for position, shards_of in pieces:
        heights = jax.random.uniform(jax.random.fold_in(jax.random.fold_in(rng, 6), position), (shards_of,), jnp.float32, low / len(pieces), top_value / len(pieces))
        gain = gain * jnp.repeat(jnp.exp(heights), shape[position] // shards_of).reshape((-1,) + (1,) * (len(shape) - 1 - position))
    return gain


def different_ones(rng, rows, number_of, top, lift):
    order = jax.random.permutation(jax.random.fold_in(rng, 1), number_of)
    pull = order
    for power in range(3):
        pull = pull * pull // number_of
    pull = pull * lift // number_of
    tickets = jax.random.randint(jax.random.fold_in(rng, 2), (rows, number_of), 0, 4096) + pull
    holders = jax.random.permutation(jax.random.fold_in(rng, 3), rows)[jnp.arange(number_of) % rows]
    tickets = jnp.where(jnp.arange(rows)[:, None] == holders[None, :], 1 << 14, tickets)
    priority = tickets * number_of + jnp.arange(number_of)
    return lax.top_k(priority.astype(jnp.int32), top)[1].astype(jnp.int32)


def noise(rng, shape, deviation, bound, shards=(), kind=jnp.bfloat16):
    level = levels(rng, shape, shards, -0.22, 0.18) if shards else 1.0
    result = jax.random.normal(rng, shape, jnp.float32) * deviation * level
    return jnp.minimum(jnp.maximum(result, -bound), bound).astype(kind)


def noise_with(rng, dims, deviation, reach, split, heavy, kind=jnp.bfloat16):
    values = deviation * jax.random.normal(rng, dims, jnp.float32)
    if split:
        values = values * levels(rng, dims, split, -0.22, 0.18)
    return jnp.clip(with_spikes(values, jax.random.fold_in(rng, 3), *heavy), -reach, reach).astype(kind)


def setup_inputs(seed: int = 0) -> dict:
    key_of = jax.random.split(jax.random.key(seed), 15)
    return {
        "question_emb": noise(key_of[0], (QUESTIONS, E), 1.0, 6.0, ((0, 128),)),
        "probes": different_ones(key_of[1], QUESTIONS, CLUSTERS, NPROBE, 1024),
        "codes": noise(key_of[2], (CLUSTERS, CSIZE, E), E ** -0.5, 0.21875, ((0, 16),)),
        "code_scale": jnp.clip(jnp.exp(math.log(4.0) - 2.7725887 * jax.random.uniform(key_of[3], (CLUSTERS, CSIZE), jnp.float32) ** levels(key_of[3], (CLUSTERS, CSIZE), ((0, 16),), -0.2, 0.2)), 0.25, 4.0),
        "question_state": noise(key_of[4], (QUESTIONS, D), 1.0, 6.0, ((0, 128),)),
        "top_passages": draw_top_passages(jax.random.fold_in(key_of[14], 71), 0),
        "soft_weight": jnp.clip(jnp.exp(math.log(0.5) - 3.218876 * jax.random.uniform(key_of[6], (QUESTIONS, TOPK), jnp.float32) ** levels(key_of[6], (QUESTIONS, TOPK), ((0, 128),), -0.2, 0.2)), 0.02, 0.5),
        "passage_home": draw_passage_home(jax.random.fold_in(key_of[14], 71), 0),
        "passage_states": noise(key_of[8], (PASSAGES, LP, D), 1.0, 6.0, ((0, 16),)),
        "norm_gain": jnp.clip(1.0 + 0.15 * jax.random.normal(key_of[9], (D,), jnp.float32), 0.25, 1.75),
        "w_gate": noise(key_of[10], (D, FW), D ** -0.5, 0.125, ((1, 16),)),
        "w_up": noise(key_of[11], (D, FW), D ** -0.5, 0.125, ((1, 16),)),
        "w_out": noise(key_of[12], (FW, D), FW ** -0.5, 0.09375, ((0, 16),)),
        "cotangent": noise_with(key_of[13], (QUESTIONS, TOPK, LP, D), 0.05, 3.0, ((0, 128),), (0, 3, 128, 5.5)),
    }


GELU_C = math.sqrt(2.0 / math.pi)

def gelu_tanh(pre_act):
    inner = GELU_C * (pre_act + 0.044715 * pre_act * pre_act * pre_act)
    return 0.5 * pre_act * (1.0 + jnp.tanh(inner))

def gelu_slope(pre_act):
    inner = GELU_C * (pre_act + 0.044715 * pre_act * pre_act * pre_act)
    tanh_val = jnp.tanh(inner)
    return 0.5 * (1.0 + tanh_val) + 0.5 * pre_act * (1.0 - tanh_val * tanh_val) * GELU_C * (1.0 + 3.0 * 0.044715 * pre_act * pre_act)

def reference(question_emb, probes, codes, code_scale, question_state, top_passages, soft_weight, passage_home, passage_states, norm_gain, w_gate, w_up, w_out, cotangent):

    def score_one(packed):
        query_vec, probe_list = packed
        blocks = codes[probe_list].astype(jnp.float32)
        scales = code_scale[probe_list]
        return jnp.einsum('e,pse->ps', query_vec.astype(jnp.float32), blocks) * scales
    probe_scores = lax.map(score_one, (question_emb, probes))
    fetched = passage_states[passage_home[top_passages]]
    inputs = fetched.astype(jnp.float32) + question_state.astype(jnp.float32)[:, None, None, :]
    inputs = inputs.reshape(-1, D)
    inverse_rms = lax.rsqrt(lax.optimization_barrier(jnp.mean(inputs * inputs, axis=-1, keepdims=True)) + 1e-06)
    normed = (inputs * inverse_rms * norm_gain).astype(jnp.bfloat16)
    gate_pre = jnp.dot(normed, w_gate, preferred_element_type=jnp.float32)
    up_pre = jnp.dot(normed, w_up, preferred_element_type=jnp.float32)
    activ = (gelu_tanh(gate_pre) * up_pre).astype(jnp.bfloat16)
    weighted = soft_weight[:, :, None, None] * cotangent.astype(jnp.float32)
    grad_rows = weighted.reshape(-1, D).astype(jnp.bfloat16)
    grad_out = jnp.dot(activ.T, grad_rows, preferred_element_type=jnp.float32)
    d_act = jnp.dot(grad_rows, w_out.T, preferred_element_type=jnp.float32)
    d_gate = (d_act * up_pre * gelu_slope(gate_pre)).astype(jnp.bfloat16)
    d_up = (d_act * gelu_tanh(gate_pre)).astype(jnp.bfloat16)
    d_normed = jnp.dot(d_gate, w_gate.T, preferred_element_type=jnp.float32) + jnp.dot(d_up, w_up.T, preferred_element_type=jnp.float32)
    grad_gain = lax.optimization_barrier(jnp.sum(d_normed * inputs * inverse_rms, axis=0))
    return (probe_scores, grad_out, grad_gain)
```

```python
import functools
import math

import jax
import jax.numpy as jnp
from jax import lax
from jax.experimental import pallas as pl
from jax.experimental.pallas import tpu as pltpu
from jax.sharding import PartitionSpec as P

BF16 = jnp.bfloat16
F32 = jnp.float32
I32 = jnp.int32

CAP = 3
NI = 16
NR = 8
TOPK = 20
NPROBE = 32
LP = 8
D = 2048
FS = 256
ROWS = TOPK * LP
PASS_DEV = 256
CLUS_DEV = 32
GELU_C = math.sqrt(2.0 / math.pi)
BOTH = ("index", "reader")


def pairs_of(move):
    pairs = []
    for x in range(4):
        for z in range(4):
            for y in range(4):
                for c in range(2):
                    tx, tz = move(x, z, c)
                    pairs.append(((x * 4 + z) * 8 + y * 2 + c, (tx * 4 + tz) * 8 + y * 2 + c))
    return pairs


def ring_move(step):
    return lambda x, z, c: ((x + step) % 4, z) if c == 0 else (x, (z + step) % 4)


def pair_move(x, z, c):
    return (x, z ^ 1) if c == 0 else (x ^ 1, z)


def partner_move(x, z, c):
    return (x, 3 - z) if c == 0 else (3 - x, z)


def ring(v, step):
    return lax.ppermute(v, BOTH, pairs_of(ring_move(step)))


def pair(v):
    return lax.ppermute(v, BOTH, pairs_of(pair_move))


def partner(v):
    return lax.ppermute(v, BOTH, pairs_of(partner_move))


def plan_kernel(top_ref, probes_ref, home_ref, emb_ref, msg_ref, src_ref):
    shape = (NI, 8, 128)
    owner_id = lax.broadcasted_iota(I32, shape, 0)
    lane_id = lax.broadcasted_iota(I32, shape, 2)
    row_id = lax.broadcasted_iota(I32, shape, 1)
    vec = jnp.where(lane_id >= 8, 64, 0)
    owners = []
    for k in range(TOPK):
        loc = home_ref[top_ref[0, k]]
        owner = loc // PASS_DEV
        rank = jnp.int32(0)
        for earlier in owners:
            rank = rank + jnp.where(earlier == owner, 1, 0)
        owners.append(owner)
        src_ref[0, k] = owner * CAP + rank
        vec = jnp.where((owner_id == owner) & (lane_id == rank), loc % PASS_DEV, vec)
    for k in range(NPROBE):
        c = probes_ref[0, k]
        vec = jnp.where((owner_id == c // CLUS_DEV) & (lane_id == 8 + k), c % CLUS_DEV, vec)
    emb = jnp.broadcast_to(emb_ref[...][None], shape)
    msg_ref[...] = jnp.where(row_id == 6, vec.astype(F32), emb).astype(BF16)


def make_plan(top, probes, home, emb):
    emb8 = jnp.pad(emb.astype(F32).reshape(6, 128), ((0, 2), (0, 0)))
    smem = pl.BlockSpec(memory_space=pltpu.SMEM)
    vmem = pl.BlockSpec(memory_space=pltpu.VMEM)
    return pl.pallas_call(
        plan_kernel,
        out_shape=(
            jax.ShapeDtypeStruct((NI, 8, 128), BF16),
            jax.ShapeDtypeStruct((1, TOPK), I32),
        ),
        in_specs=[smem, smem, smem, vmem],
        out_specs=(vmem, smem),
        name="plan",
    )(top, probes, home, emb8)


def pick_kernel(slot_ref, states_ref, out_ref, sems):
    copies = []
    for i in range(NI * CAP):
        row = slot_ref[i // CAP, i % CAP]
        copy = pltpu.make_async_copy(states_ref.at[row], out_ref.at[i], sems.at[i])
        copy.start()
        copies.append(copy)
    for copy in copies:
        copy.wait()


def pick_slots(slots, states):
    return pl.pallas_call(
        pick_kernel,
        out_shape=jax.ShapeDtypeStruct((NI * CAP, LP, D), BF16),
        in_specs=[pl.BlockSpec(memory_space=pltpu.SMEM), pl.BlockSpec(memory_space=pl.ANY)],
        out_specs=pl.BlockSpec(memory_space=pl.ANY),
        scratch_shapes=[pltpu.SemaphoreType.DMA((NI * CAP,))],
        cost_estimate=pl.CostEstimate(flops=0, bytes_accessed=2 * NI * CAP * LP * D * 2, transcendentals=0),
        name="pick",
    )(slots, states)


def norm_kernel(src_ref, recv_ref, state_ref, gain_ref, out_ref, buf, sems):
    copies = []
    for k in range(TOPK):
        copy = pltpu.make_async_copy(recv_ref.at[src_ref[0, k]], buf.at[k], sems.at[k])
        copy.start()
        copies.append(copy)
    state = state_ref[...].astype(F32)
    gain = gain_ref[...]
    for k in range(TOPK // 2):
        copies[2 * k].wait()
        copies[2 * k + 1].wait()
        x = buf[2 * k : 2 * k + 2].astype(F32).reshape(2 * LP, D) + state
        inv = lax.rsqrt(jnp.mean(x * x, axis=-1, keepdims=True) + 1e-06)
        out_ref[2 * LP * k : 2 * LP * (k + 1), :] = (x * inv * gain).astype(BF16)


def norm_rows(src, recv, state, gain):
    vmem = pl.BlockSpec(memory_space=pltpu.VMEM)
    return pl.pallas_call(
        norm_kernel,
        out_shape=jax.ShapeDtypeStruct((ROWS, D), BF16),
        in_specs=[
            pl.BlockSpec(memory_space=pltpu.SMEM),
            pl.BlockSpec(memory_space=pl.ANY),
            vmem,
            vmem,
        ],
        out_specs=vmem,
        scratch_shapes=[pltpu.VMEM((TOPK, LP, D), BF16), pltpu.SemaphoreType.DMA((TOPK,))],
        name="norm",
    )(src, recv, state, gain)


NT = (((1,), (1,)), ((), ()))


def layer_kernel(blocks, tile, last, *refs):
    n_in = refs[:blocks]
    d_in = refs[blocks : 2 * blocks]
    wg_in, wu_in, wo_in, wp_in = refs[2 * blocks : 2 * blocks + 4]
    rest = refs[2 * blocks + 4 :]
    if last:
        acc_in, gacc_ref, gain_ref, own_ref, par_ref, gout_ref = rest[:6]
        rest = rest[6:]
    else:
        acc_ref, gout_ref = rest[:2]
        rest = rest[2:]
    nbuf, dbuf, wg, wu, wo, act, dgate, dup = rest[:8]
    rest = rest[8:]
    if last:
        acc_ref = rest[0]
        rest = rest[1:]
    sems = rest[0]
    count = [0]

    def start(src, dst):
        copy = pltpu.make_async_copy(src, dst, sems.at[count[0]])
        count[0] += 1
        copy.start()
        return copy

    first, second, third = [], [], []
    first.append(start(wg_in, wg.at[:, pl.ds(0, FS)]))
    first.append(start(wu_in, wu.at[:, pl.ds(0, FS)]))
    for j in range(4):
        first.append(start(wp_in.at[pl.ds(j * 1536, 512)], wg.at[pl.ds(j * 512, 512), pl.ds(FS, FS)]))
        first.append(start(wp_in.at[pl.ds(j * 1536 + 512, 512)], wu.at[pl.ds(j * 512, 512), pl.ds(FS, FS)]))
    for b in range(blocks):
        first.append(start(n_in[b], nbuf.at[pl.ds(b * ROWS, ROWS)]))
    second.append(start(wo_in, wo.at[pl.ds(0, FS)]))
    for j in range(4):
        for h in range(2):
            second.append(
                start(
                    wp_in.at[pl.ds(j * 1536 + 1024 + h * FS, FS)],
                    wo.at[pl.ds(FS, FS), pl.ds(j * 512 + h * FS, FS)],
                )
            )
    for b in range(blocks):
        second.append(start(d_in[b], dbuf.at[pl.ds(b * ROWS, ROWS)]))
    if last:
        third.append(start(acc_in, acc_ref))
    for copy in first + second:
        copy.wait()

    def body(t, carry):
        rows = pl.ds(pl.multiple_of(t * tile, 16), tile)
        n = nbuf[rows, :]
        gate = jnp.dot(n, wg[...], preferred_element_type=F32)
        up = jnp.dot(n, wu[...], preferred_element_type=F32)
        d_act = lax.dot_general(dbuf[rows, :], wo[...], NT, preferred_element_type=F32)
        inner = GELU_C * (gate + 0.044715 * gate * gate * gate)
        th = jnp.tanh(inner)
        half = 0.5 * (1.0 + th)
        gelu = gate * half
        slope = half + 0.5 * gate * (1.0 - th * th) * GELU_C * (1.0 + 3.0 * 0.044715 * gate * gate)
        act[rows, :] = (gelu * up).astype(BF16)
        dgate[rows, :] = (d_act * up * slope).astype(BF16)
        dup[rows, :] = (d_act * gelu).astype(BF16)
        return carry

    lax.fori_loop(0, blocks * ROWS // tile, body, 0)

    def gain_body(j, carry):
        cols = pl.ds(pl.multiple_of(j * 512, 512), 512)
        dn = lax.dot_general(dgate[...], wg[cols, :], NT, preferred_element_type=F32)
        dn = dn + lax.dot_general(dup[...], wu[cols, :], NT, preferred_element_type=F32)
        part = jnp.sum(dn * nbuf[:, cols].astype(F32), axis=0, keepdims=True)
        if last:
            part = (part + gacc_ref[:, cols]) / gain_ref[:, cols]
        gout_ref[:, cols] = part
        return carry

    lax.fori_loop(0, 4, gain_body, 0)
    for copy in third:
        copy.wait()
    act_t = act[...].T

    def out_body(r, carry):
        cols = pl.ds(pl.multiple_of(r * FS, FS), FS)
        part = jnp.dot(act_t, dbuf[:, cols], preferred_element_type=F32)
        if last:
            part = part + acc_ref[r]
            own_ref[r] = part[:FS]
            par_ref[r] = part[FS:].astype(BF16)
        else:
            acc_ref[r] = part
        return carry

    lax.fori_loop(0, NR, out_body, 0)


def layer(n_blocks, d_blocks, weights, tile, carried=None):
    blocks = len(n_blocks)
    rows = blocks * ROWS
    last = carried is not None
    any_ = pl.BlockSpec(memory_space=pl.ANY)
    vmem = pl.BlockSpec(memory_space=pltpu.VMEM)
    args = [*n_blocks, *d_blocks, *weights]
    in_specs = [any_] * len(args)
    if last:
        args += list(carried)
        in_specs += [any_, vmem, vmem]
        out_shape = (
            jax.ShapeDtypeStruct((NR, FS, FS), F32),
            jax.ShapeDtypeStruct((NR, FS, FS), BF16),
            jax.ShapeDtypeStruct((1, D), F32),
        )
    else:
        out_shape = (
            jax.ShapeDtypeStruct((NR, 2 * FS, FS), F32),
            jax.ShapeDtypeStruct((1, D), F32),
        )
    scratch = [
        pltpu.VMEM((rows, D), BF16),
        pltpu.VMEM((rows, D), BF16),
        pltpu.VMEM((D, 2 * FS), BF16),
        pltpu.VMEM((D, 2 * FS), BF16),
        pltpu.VMEM((2 * FS, D), BF16),
        pltpu.VMEM((rows, 2 * FS), BF16),
        pltpu.VMEM((rows, 2 * FS), BF16),
        pltpu.VMEM((rows, 2 * FS), BF16),
    ]
    if last:
        scratch.append(pltpu.VMEM((NR, 2 * FS, FS), F32))
    scratch.append(pltpu.SemaphoreType.DMA((2 * blocks + 20,)))
    return pl.pallas_call(
        functools.partial(layer_kernel, blocks, tile, last),
        out_shape=out_shape,
        in_specs=in_specs,
        out_specs=tuple(vmem for _ in out_shape),
        scratch_shapes=scratch,
        compiler_params=pltpu.CompilerParams(vmem_limit_bytes=40 * 1024 * 1024),
        cost_estimate=pl.CostEstimate(
            flops=12 * rows * D * 2 * FS, bytes_accessed=4 * rows * D + 6 * D * 2 * FS, transcendentals=rows * 512
        ),
        name="layer_last" if last else "layer_first",
    )(*args)


def shards(
    question_emb,
    probes,
    codes,
    code_scale,
    question_state,
    top_passages,
    soft_weight,
    passage_home,
    passage_states,
    norm_gain,
    w_gate,
    w_up,
    w_out,
    cotangent,
):
    dy0 = (soft_weight[:, :, None, None] * cotangent.astype(F32)).astype(BF16).reshape(ROWS, D)
    dyp = pair(dy0)
    dy_a = [dy0, ring(dy0, 1), ring(dy0, -1), ring(dy0, 2), dyp]
    y = lax.axis_index("reader") // 2
    piece = jnp.concatenate(
        [
            lax.dynamic_slice(w_gate, (y * 512, 0), (512, FS)),
            lax.dynamic_slice(w_up, (y * 512, 0), (512, FS)),
            lax.dynamic_slice(w_out, (0, y * 512), (FS, FS)),
            lax.dynamic_slice(w_out, (0, y * 512 + FS), (FS, FS)),
        ],
        axis=0,
    )
    piece = partner(piece)
    wp = lax.all_gather(
        piece, "reader", axis=0, tiled=True, axis_index_groups=[[0, 2, 4, 6], [1, 3, 5, 7]]
    )
    weights = (w_gate, w_up, w_out, wp)

    msg, src = make_plan(top_passages, probes, passage_home, question_emb)
    asked = lax.all_to_all(msg, "index", 0, 0, tiled=True)
    slots = asked[:, 6, :CAP].astype(I32)
    blocks = pick_slots(slots, passage_states)
    recv = lax.all_to_all(blocks, "index", 0, 0, tiled=True)
    gain_row = norm_gain.reshape(1, D)
    n0 = norm_rows(src, recv, question_state, gain_row)

    dy_b = [ring(dyp, 1), ring(dyp, -1), ring(dyp, 2)]
    np_ = pair(n0)
    n_a = [n0, ring(n0, 1), ring(n0, -1), ring(n0, 2), np_]
    n_b = [ring(np_, 1), ring(np_, -1), ring(np_, 2)]

    group_emb = asked[:, :6, :].reshape(NI, 768)
    every_score = (
        jnp.einsum("qe,cse->qcs", group_emb, codes, preferred_element_type=F32) * code_scale[None]
    )
    local = asked[:, 6, 8 : 8 + NPROBE].astype(I32)
    hot = (local[:, :, None] == jnp.arange(CLUS_DEV, dtype=I32)[None, None, :]).astype(F32)
    picked = jnp.einsum("qpc,qcs->qps", hot, every_score, precision=lax.Precision.HIGHEST)

    acc_a, gain_a = layer(n_a, dy_a, weights, 400)
    own, par, gain_part = layer(n_b, dy_b, weights, 240, (acc_a, gain_a, gain_row))

    from_partner = partner(par)
    tail = jnp.concatenate(
        [picked, gain_part.reshape(NI, 1, 128), jnp.zeros((NI, 7, 128), F32)], axis=1
    )
    tail = lax.all_to_all(tail, "index", 0, 0, tiled=True)
    tail = jnp.sum(tail, axis=0)
    probe_scores = tail[None, :NPROBE]
    gain128 = tail[NPROBE].reshape(NR, 1, 16)
    hi = gain128.astype(BF16)
    lo = (gain128 - hi.astype(F32)).astype(BF16)
    gain_rows = jnp.pad(jnp.concatenate([hi, lo], axis=2), ((0, 0), (0, 7), (0, FS - 32)))
    total = (own + from_partner.astype(F32)).astype(BF16)
    out = lax.all_to_all(jnp.concatenate([total, gain_rows], axis=1), "reader", 0, 0, tiled=True)
    out = jnp.sum(out.astype(F32), axis=0)
    grad_out = out[:FS]
    grad_gain = out[FS, :16] + out[FS, 16:32]
    return probe_scores, grad_out, grad_gain


def solution(mesh):
    return jax.shard_map(
        shards,
        mesh=mesh,
        in_specs=(
            P(("index", "reader"), None),
            P(("index", "reader"), None),
            P("index", None, None),
            P("index", None),
            P(("index", "reader"), None),
            P(("index", "reader"), None),
            P(("index", "reader"), None),
            P(),
            P("index", None, None),
            P(),
            P(None, "index"),
            P(None, "index"),
            P("index", None),
            P(("index", "reader"), None, None, None),
        ),
        out_specs=(
            P(("index", "reader"), None, None),
            P("index", "reader"),
            P(("index", "reader")),
        ),
        check_vma=False,
    )
```

```python
import functools
import math

import jax
import jax.numpy as jnp
from jax import lax
from jax.experimental import pallas as pl
from jax.experimental.pallas import tpu as pltpu
from jax.sharding import PartitionSpec as P

BF16 = jnp.bfloat16
F32 = jnp.float32
I32 = jnp.int32

CAP = 3
NI = 16
NR = 8
TOPK = 20
NPROBE = 32
LP = 8
D = 2048
FS = 256
ROWS = TOPK * LP
PASS_DEV = 256
CLUS_DEV = 32
GELU_C = math.sqrt(2.0 / math.pi)
BOTH = ("index", "reader")


def pairs_of(move):
    pairs = []
    for x in range(4):
        for z in range(4):
            for y in range(4):
                for c in range(2):
                    tx, tz = move(x, z, c)
                    pairs.append(((x * 4 + z) * 8 + y * 2 + c, (tx * 4 + tz) * 8 + y * 2 + c))
    return pairs


def ring_move(step):
    return lambda x, z, c: ((x + step) % 4, z) if c == 0 else (x, (z + step) % 4)


def pair_move(x, z, c):
    return (x, z ^ 1) if c == 0 else (x ^ 1, z)


def partner_move(x, z, c):
    return (x, 3 - z) if c == 0 else (3 - x, z)


def column_pairs(step):
    pairs = []
    for i in range(NI):
        for y in range(4):
            for c in range(2):
                pairs.append((i * 8 + y * 2 + c, i * 8 + (y + step) % 4 * 2 + c))
    return pairs


def column(v, step):
    return lax.ppermute(v, BOTH, column_pairs(step))


def ring(v, step):
    return lax.ppermute(v, BOTH, pairs_of(ring_move(step)))


def pair(v):
    return lax.ppermute(v, BOTH, pairs_of(pair_move))


def partner(v):
    return lax.ppermute(v, BOTH, pairs_of(partner_move))


def plan_kernel(top_ref, probes_ref, home_ref, emb_ref, msg_ref, src_ref):
    shape = (NI, 8, 128)
    owner_id = lax.broadcasted_iota(I32, shape, 0)
    lane_id = lax.broadcasted_iota(I32, shape, 2)
    row_id = lax.broadcasted_iota(I32, shape, 1)
    vec = jnp.where(lane_id >= 8, 64, 0)
    owners = []
    for k in range(TOPK):
        loc = home_ref[top_ref[0, k]]
        owner = loc // PASS_DEV
        rank = jnp.int32(0)
        for earlier in owners:
            rank = rank + jnp.where(earlier == owner, 1, 0)
        owners.append(owner)
        src_ref[0, k] = owner * CAP + rank
        vec = jnp.where((owner_id == owner) & (lane_id == rank), loc % PASS_DEV, vec)
    for k in range(NPROBE):
        c = probes_ref[0, k]
        vec = jnp.where((owner_id == c // CLUS_DEV) & (lane_id == 8 + k), c % CLUS_DEV, vec)
    emb = jnp.broadcast_to(emb_ref[...][None], shape)
    msg_ref[...] = jnp.where(row_id == 6, vec.astype(F32), emb).astype(BF16)


def make_plan(top, probes, home, emb):
    emb8 = jnp.pad(emb.astype(F32).reshape(6, 128), ((0, 2), (0, 0)))
    smem = pl.BlockSpec(memory_space=pltpu.SMEM)
    vmem = pl.BlockSpec(memory_space=pltpu.VMEM)
    return pl.pallas_call(
        plan_kernel,
        out_shape=(
            jax.ShapeDtypeStruct((NI, 8, 128), BF16),
            jax.ShapeDtypeStruct((1, TOPK), I32),
        ),
        in_specs=[smem, smem, smem, vmem],
        out_specs=(vmem, smem),
        name="plan",
    )(top, probes, home, emb8)


def pick_kernel(slot_ref, states_ref, *refs):
    out_ref, sems = refs[(len(refs) - 2) // 2], refs[-1]
    copies = []
    for i in range(NI * CAP):
        row = slot_ref[i // CAP, i % CAP]
        copy = pltpu.make_async_copy(states_ref.at[row], out_ref.at[i], sems.at[i])
        copy.start()
        copies.append(copy)
    for copy in copies:
        copy.wait()


def pick_slots(slots, states, *passed):
    any_ = pl.BlockSpec(memory_space=pl.ANY)
    return pl.pallas_call(
        pick_kernel,
        out_shape=(
            jax.ShapeDtypeStruct((NI * CAP, LP, D), BF16),
            *(jax.ShapeDtypeStruct(v.shape, v.dtype) for v in passed),
        ),
        in_specs=[pl.BlockSpec(memory_space=pltpu.SMEM), any_] + [any_] * len(passed),
        out_specs=(pl.BlockSpec(memory_space=pltpu.VMEM), *(any_ for _ in passed)),
        input_output_aliases={2 + i: 1 + i for i in range(len(passed))},
        scratch_shapes=[pltpu.SemaphoreType.DMA((NI * CAP,))],
        compiler_params=pltpu.CompilerParams(vmem_limit_bytes=57 * 1024 * 1024),
        cost_estimate=pl.CostEstimate(flops=0, bytes_accessed=2 * NI * CAP * LP * D * 2, transcendentals=0),
        name="pick",
    )(slots, states, *passed)


def norm_kernel(src_ref, recv_ref, state_ref, gain_ref, *refs):
    out_ref, buf, sems = refs[-3:]
    copies = []
    for k in range(TOPK):
        copy = pltpu.make_async_copy(recv_ref.at[src_ref[0, k]], buf.at[k], sems.at[k])
        copy.start()
        copies.append(copy)
    state = state_ref[...].astype(F32)
    gain = gain_ref[...]
    for k in range(TOPK // 2):
        copies[2 * k].wait()
        copies[2 * k + 1].wait()
        x = buf[2 * k : 2 * k + 2].astype(F32).reshape(2 * LP, D) + state
        inv = lax.rsqrt(jnp.mean(x * x, axis=-1, keepdims=True) + 1e-06)
        out_ref[2 * LP * k : 2 * LP * (k + 1), :] = (x * inv * gain).astype(BF16)


def norm_rows(src, recv, state, gain, *after):
    vmem = pl.BlockSpec(memory_space=pltpu.VMEM)
    return pl.pallas_call(
        norm_kernel,
        out_shape=jax.ShapeDtypeStruct((ROWS, D), BF16),
        in_specs=[
            pl.BlockSpec(memory_space=pltpu.SMEM),
            pl.BlockSpec(memory_space=pl.ANY),
            vmem,
            vmem,
            *(pl.BlockSpec(memory_space=pl.ANY) for _ in after),
        ],
        out_specs=vmem,
        scratch_shapes=[pltpu.VMEM((TOPK, LP, D), BF16), pltpu.SemaphoreType.DMA((TOPK,))],
        compiler_params=pltpu.CompilerParams(vmem_limit_bytes=8 * 1024 * 1024),
        name="norm",
    )(src, recv, state, gain, *after)


NT = (((1,), (1,)), ((), ()))


def layer_kernel(blocks, tile, last, *refs):
    y = refs[0][0, 0]
    refs = refs[1:]
    n_in = refs[:blocks]
    d_in = refs[blocks : 2 * blocks]
    wg_in, wu_in, wo_in = refs[2 * blocks : 2 * blocks + 3]
    wp_in = refs[2 * blocks + 3 : 2 * blocks + 7]
    rest = refs[2 * blocks + 7 :]
    if last:
        acc_in, gacc_ref, gain_ref, own_ref, par_ref, gout_ref = rest[:6]
        rest = rest[6:]
    else:
        acc_ref, gout_ref = rest[:2]
        rest = rest[2:]
    nbuf, dbuf, wg, wu, wo, act, dgate, dup = rest[:8]
    rest = rest[8:]
    if last:
        acc_ref = rest[0]
        rest = rest[1:]
    sems = rest[0]
    count = [0]

    def start(src, dst):
        copy = pltpu.make_async_copy(src, dst, sems.at[count[0]])
        count[0] += 1
        copy.start()
        return copy

    first, second, third = [], [], []
    first.append(start(wg_in, wg.at[:, pl.ds(0, FS)]))
    first.append(start(wu_in, wu.at[:, pl.ds(0, FS)]))
    for j in range(4):
        part = pl.multiple_of((y + j) % 4 * 512, 512)
        first.append(start(wp_in[j].at[pl.ds(0, 512)], wg.at[pl.ds(part, 512), pl.ds(FS, FS)]))
        first.append(start(wp_in[j].at[pl.ds(512, 512)], wu.at[pl.ds(part, 512), pl.ds(FS, FS)]))
    for b in range(blocks):
        first.append(start(n_in[b], nbuf.at[pl.ds(b * ROWS, ROWS)]))
    second.append(start(wo_in, wo.at[pl.ds(0, FS)]))
    for j in range(4):
        for h in range(2):
            part = pl.multiple_of((y + j) % 4 * 512 + h * FS, FS)
            second.append(
                start(wp_in[j].at[pl.ds(1024 + h * FS, FS)], wo.at[pl.ds(FS, FS), pl.ds(part, FS)])
            )
    for b in range(blocks):
        second.append(start(d_in[b], dbuf.at[pl.ds(b * ROWS, ROWS)]))
    if last:
        third.append(start(acc_in, acc_ref))
    for copy in first + second:
        copy.wait()

    def body(t, carry):
        rows = pl.ds(pl.multiple_of(t * tile, 16), tile)
        n = nbuf[rows, :]
        gate = jnp.dot(n, wg[...], preferred_element_type=F32)
        up = jnp.dot(n, wu[...], preferred_element_type=F32)
        d_act = lax.dot_general(dbuf[rows, :], wo[...], NT, preferred_element_type=F32)
        inner = GELU_C * (gate + 0.044715 * gate * gate * gate)
        th = jnp.tanh(inner)
        half = 0.5 * (1.0 + th)
        gelu = gate * half
        slope = half + 0.5 * gate * (1.0 - th * th) * GELU_C * (1.0 + 3.0 * 0.044715 * gate * gate)
        act[rows, :] = (gelu * up).astype(BF16)
        dgate[rows, :] = (d_act * up * slope).astype(BF16)
        dup[rows, :] = (d_act * gelu).astype(BF16)
        return carry

    lax.fori_loop(0, blocks * ROWS // tile, body, 0)

    def gain_body(j, carry):
        cols = pl.ds(pl.multiple_of(j * 512, 512), 512)
        dn = lax.dot_general(dgate[...], wg[cols, :], NT, preferred_element_type=F32)
        dn = dn + lax.dot_general(dup[...], wu[cols, :], NT, preferred_element_type=F32)
        part = jnp.sum(dn * nbuf[:, cols].astype(F32), axis=0, keepdims=True)
        if last:
            part = (part + gacc_ref[:, cols]) / gain_ref[:, cols]
        gout_ref[:, cols] = part
        return carry

    lax.fori_loop(0, 4, gain_body, 0)
    for copy in third:
        copy.wait()
    act_t = act[...].T

    def out_body(r, carry):
        cols = pl.ds(pl.multiple_of(r * FS, FS), FS)
        part = jnp.dot(act_t, dbuf[:, cols], preferred_element_type=F32)
        if last:
            part = part + acc_ref[r]
            own_ref[r] = part[:FS]
            par_ref[r] = part[FS:].astype(BF16)
        else:
            acc_ref[r] = part
        return carry

    lax.fori_loop(0, NR, out_body, 0)


def layer(y, n_blocks, d_blocks, weights, tile, carried=None):
    blocks = len(n_blocks)
    rows = blocks * ROWS
    last = carried is not None
    any_ = pl.BlockSpec(memory_space=pl.ANY)
    vmem = pl.BlockSpec(memory_space=pltpu.VMEM)
    args = [y, *n_blocks, *d_blocks, *weights]
    in_specs = [pl.BlockSpec(memory_space=pltpu.SMEM)] + [any_] * (len(args) - 1)
    if last:
        args += list(carried)
        in_specs += [any_, vmem, vmem]
        out_shape = (
            jax.ShapeDtypeStruct((NR, FS, FS), F32),
            jax.ShapeDtypeStruct((NR, FS, FS), BF16),
            jax.ShapeDtypeStruct((1, D), F32),
        )
    else:
        out_shape = (
            jax.ShapeDtypeStruct((NR, 2 * FS, FS), F32),
            jax.ShapeDtypeStruct((1, D), F32),
        )
    scratch = [
        pltpu.VMEM((rows, D), BF16),
        pltpu.VMEM((rows, D), BF16),
        pltpu.VMEM((D, 2 * FS), BF16),
        pltpu.VMEM((D, 2 * FS), BF16),
        pltpu.VMEM((2 * FS, D), BF16),
        pltpu.VMEM((rows, 2 * FS), BF16),
        pltpu.VMEM((rows, 2 * FS), BF16),
        pltpu.VMEM((rows, 2 * FS), BF16),
    ]
    if last:
        scratch.append(pltpu.VMEM((NR, 2 * FS, FS), F32))
    scratch.append(pltpu.SemaphoreType.DMA((2 * blocks + 20,)))
    return pl.pallas_call(
        functools.partial(layer_kernel, blocks, tile, last),
        out_shape=out_shape,
        in_specs=in_specs,
        out_specs=tuple(vmem for _ in out_shape),
        scratch_shapes=scratch,
        compiler_params=pltpu.CompilerParams(vmem_limit_bytes=60 * 1024 * 1024),
        cost_estimate=pl.CostEstimate(
            flops=12 * rows * D * 2 * FS, bytes_accessed=4 * rows * D + 6 * D * 2 * FS, transcendentals=rows * 512
        ),
        name="layer_last" if last else "layer_first",
    )(*args)


def shards(
    question_emb,
    probes,
    codes,
    code_scale,
    question_state,
    top_passages,
    soft_weight,
    passage_home,
    passage_states,
    norm_gain,
    w_gate,
    w_up,
    w_out,
    cotangent,
):
    dy0 = (soft_weight[:, :, None, None] * cotangent.astype(F32)).astype(BF16).reshape(ROWS, D)
    dyp = pair(dy0)
    dy_next = ring(dy0, 1)
    dy_prev = ring(dy0, -1)
    y = lax.axis_index("reader") // 2
    y_row = y.astype(I32).reshape(1, 1)
    piece = jnp.concatenate(
        [
            lax.dynamic_slice(w_gate, (y * 512, 0), (512, FS)),
            lax.dynamic_slice(w_up, (y * 512, 0), (512, FS)),
            lax.dynamic_slice(w_out, (0, y * 512), (FS, FS)),
            lax.dynamic_slice(w_out, (0, y * 512 + FS), (FS, FS)),
        ],
        axis=0,
    )
    piece = partner(piece)

    msg, src = make_plan(top_passages, probes, passage_home, question_emb)
    asked = lax.all_to_all(msg, "index", 0, 0, tiled=True)
    slots = asked[:, 6, :CAP].astype(I32)
    blocks, piece, dyp, dy_next, dy_prev = pick_slots(
        slots, passage_states, piece, dyp, dy_next, dy_prev
    )
    recv = lax.all_to_all(blocks, "index", 0, 0, tiled=True)
    dy_far = ring(dy0, 2)
    dy_a = [dy0, dy_next, dy_prev, dy_far, dyp]
    dy_b = [ring(dyp, 1), ring(dyp, -1), ring(dyp, 2)]
    weights = (w_gate, w_up, w_out, piece, column(piece, -1), column(piece, 2), column(piece, 1))
    gain_row = norm_gain.reshape(1, D)
    n0 = norm_rows(src, recv, question_state, gain_row, dy_far, *dy_b)
    np_ = pair(n0)
    n_a = [n0, ring(n0, 1), ring(n0, -1), ring(n0, 2), np_]
    n_b = [ring(np_, 1), ring(np_, -1), ring(np_, 2)]

    group_emb = asked[:, :6, :].reshape(NI, 768)
    every_score = (
        jnp.einsum("qe,cse->qcs", group_emb, codes, preferred_element_type=F32) * code_scale[None]
    )
    local = asked[:, 6, 8 : 8 + NPROBE].astype(I32)
    hot = (local[:, :, None] == jnp.arange(CLUS_DEV, dtype=I32)[None, None, :]).astype(F32)
    picked = jnp.einsum("qpc,qcs->qps", hot, every_score, precision=lax.Precision.HIGHEST)

    acc_a, gain_a = layer(y_row, n_a, dy_a, weights, 400)
    own, par, gain_part = layer(y_row, n_b, dy_b, weights, 240, (acc_a, gain_a, gain_row))

    from_partner = partner(par)
    tail = jnp.concatenate(
        [picked, gain_part.reshape(NI, 1, 128), jnp.zeros((NI, 7, 128), F32)], axis=1
    )
    tail = lax.all_to_all(tail, "index", 0, 0, tiled=True)
    tail = jnp.sum(tail, axis=0)
    probe_scores = tail[None, :NPROBE]
    gain128 = tail[NPROBE].reshape(NR, 1, 16)
    hi = gain128.astype(BF16)
    lo = (gain128 - hi.astype(F32)).astype(BF16)
    gain_rows = jnp.pad(jnp.concatenate([hi, lo], axis=2), ((0, 0), (0, 7), (0, FS - 32)))
    total = (own + from_partner.astype(F32)).astype(BF16)
    out = lax.all_to_all(jnp.concatenate([total, gain_rows], axis=1), "reader", 0, 0, tiled=True)
    out = jnp.sum(out.astype(F32), axis=0)
    grad_out = out[:FS]
    grad_gain = out[FS, :16] + out[FS, 16:32]
    return probe_scores, grad_out, grad_gain


def solution(mesh):
    return jax.shard_map(
        shards,
        mesh=mesh,
        in_specs=(
            P(("index", "reader"), None),
            P(("index", "reader"), None),
            P("index", None, None),
            P("index", None),
            P(("index", "reader"), None),
            P(("index", "reader"), None),
            P(("index", "reader"), None),
            P(),
            P("index", None, None),
            P(),
            P(None, "index"),
            P(None, "index"),
            P("index", None),
            P(("index", "reader"), None, None, None),
        ),
        out_specs=(
            P(("index", "reader"), None, None),
            P("index", "reader"),
            P(("index", "reader")),
        ),
        check_vma=False,
    )
```

```python
import functools
import math

import jax
import jax.numpy as jnp
from jax import lax
from jax.experimental import pallas as pl
from jax.experimental.pallas import tpu as pltpu
from jax.sharding import PartitionSpec as P

BF16 = jnp.bfloat16
F32 = jnp.float32
I32 = jnp.int32

CAP = 3
FIRST_TILE = 400
LAST_TILE = 480
READY_VMEM = 20
LAYER_VMEM = 26
NI = 16
NR = 8
TOPK = 20
NPROBE = 32
LP = 8
D = 2048
FS = 256
ROWS = TOPK * LP
PASS_DEV = 256
CLUS_DEV = 32
GELU_C = math.sqrt(2.0 / math.pi)
BOTH = ("index", "reader")


def pairs_of(move):
    pairs = []
    for x in range(4):
        for z in range(4):
            for y in range(4):
                for c in range(2):
                    tx, tz = move(x, z, c)
                    pairs.append(((x * 4 + z) * 8 + y * 2 + c, (tx * 4 + tz) * 8 + y * 2 + c))
    return pairs


def ring_move(step):
    return lambda x, z, c: ((x + step) % 4, z) if c == 0 else (x, (z + step) % 4)


def pair_move(x, z, c):
    return (x, z ^ 1) if c == 0 else (x ^ 1, z)


def partner_move(x, z, c):
    return (x, 3 - z) if c == 0 else (3 - x, z)


def column_pairs(step):
    pairs = []
    for i in range(NI):
        for y in range(4):
            for c in range(2):
                pairs.append((i * 8 + y * 2 + c, i * 8 + (y + step) % 4 * 2 + c))
    return pairs


def column(v, step):
    return lax.ppermute(v, BOTH, column_pairs(step))


def ring(v, step):
    return lax.ppermute(v, BOTH, pairs_of(ring_move(step)))


def pair(v):
    return lax.ppermute(v, BOTH, pairs_of(pair_move))


def partner(v):
    return lax.ppermute(v, BOTH, pairs_of(partner_move))


def plan_kernel(top_ref, probes_ref, home_ref, emb_ref, msg_ref, src_ref):
    shape = (NI, 8, 128)
    owner_id = lax.broadcasted_iota(I32, shape, 0)
    lane_id = lax.broadcasted_iota(I32, shape, 2)
    row_id = lax.broadcasted_iota(I32, shape, 1)
    vec = jnp.where(lane_id >= 8, 64, 0)
    owners = []
    for k in range(TOPK):
        loc = home_ref[top_ref[0, k]]
        owner = loc // PASS_DEV
        rank = jnp.int32(0)
        for earlier in owners:
            rank = rank + jnp.where(earlier == owner, 1, 0)
        owners.append(owner)
        src_ref[0, k] = owner * CAP + rank
        vec = jnp.where((owner_id == owner) & (lane_id == rank), loc % PASS_DEV, vec)
    for k in range(NPROBE):
        c = probes_ref[0, k]
        vec = jnp.where((owner_id == c // CLUS_DEV) & (lane_id == 8 + k), c % CLUS_DEV, vec)
    emb = jnp.broadcast_to(emb_ref[...][None], shape)
    msg_ref[...] = jnp.where(row_id == 6, vec.astype(F32), emb).astype(BF16)


def make_plan(top, probes, home, emb):
    emb8 = jnp.pad(emb.astype(F32).reshape(6, 128), ((0, 2), (0, 0)))
    smem = pl.BlockSpec(memory_space=pltpu.SMEM)
    vmem = pl.BlockSpec(memory_space=pltpu.VMEM)
    return pl.pallas_call(
        plan_kernel,
        out_shape=(
            jax.ShapeDtypeStruct((NI, 8, 128), BF16),
            jax.ShapeDtypeStruct((1, TOPK), I32),
        ),
        in_specs=[smem, smem, smem, vmem],
        out_specs=(vmem, smem),
        name="plan",
    )(top, probes, home, emb8)


def pick_kernel(slot_ref, states_ref, *refs):
    out_ref, sems = refs[(len(refs) - 2) // 2], refs[-1]
    copies = []
    for i in range(NI * CAP):
        row = slot_ref[i // CAP, i % CAP]
        copy = pltpu.make_async_copy(states_ref.at[row], out_ref.at[i], sems.at[i])
        copy.start()
        copies.append(copy)
    for copy in copies:
        copy.wait()


def pick_slots(slots, states, *passed):
    any_ = pl.BlockSpec(memory_space=pl.ANY)
    return pl.pallas_call(
        pick_kernel,
        out_shape=(
            jax.ShapeDtypeStruct((NI * CAP, LP, D), BF16),
            *(jax.ShapeDtypeStruct(v.shape, v.dtype) for v in passed),
        ),
        in_specs=[pl.BlockSpec(memory_space=pltpu.SMEM), any_] + [any_] * len(passed),
        out_specs=(pl.BlockSpec(memory_space=pltpu.VMEM), *(any_ for _ in passed)),
        input_output_aliases={2 + i: 1 + i for i in range(len(passed))},
        scratch_shapes=[pltpu.SemaphoreType.DMA((NI * CAP,))],
        compiler_params=pltpu.CompilerParams(vmem_limit_bytes=57 * 1024 * 1024),
        cost_estimate=pl.CostEstimate(flops=0, bytes_accessed=2 * NI * CAP * LP * D * 2, transcendentals=0),
        name="pick",
    )(slots, states, *passed)


def norm_kernel(src_ref, recv_ref, state_ref, gain_ref, *refs):
    out_ref, buf, sems = refs[-3:]
    copies = []
    for k in range(TOPK):
        copy = pltpu.make_async_copy(recv_ref.at[src_ref[0, k]], buf.at[k], sems.at[k])
        copy.start()
        copies.append(copy)
    state = state_ref[...].astype(F32)
    gain = gain_ref[...]
    for k in range(TOPK // 2):
        copies[2 * k].wait()
        copies[2 * k + 1].wait()
        x = buf[2 * k : 2 * k + 2].astype(F32).reshape(2 * LP, D) + state
        inv = lax.rsqrt(jnp.mean(x * x, axis=-1, keepdims=True) + 1e-06)
        out_ref[2 * LP * k : 2 * LP * (k + 1), :] = (x * inv * gain).astype(BF16)


def norm_rows(src, recv, state, gain, *after):
    vmem = pl.BlockSpec(memory_space=pltpu.VMEM)
    return pl.pallas_call(
        norm_kernel,
        out_shape=jax.ShapeDtypeStruct((ROWS, D), BF16),
        in_specs=[
            pl.BlockSpec(memory_space=pltpu.SMEM),
            pl.BlockSpec(memory_space=pl.ANY),
            vmem,
            vmem,
            *(pl.BlockSpec(memory_space=pl.ANY) for _ in after),
        ],
        out_specs=vmem,
        scratch_shapes=[pltpu.VMEM((TOPK, LP, D), BF16), pltpu.SemaphoreType.DMA((TOPK,))],
        compiler_params=pltpu.CompilerParams(vmem_limit_bytes=8 * 1024 * 1024),
        name="norm",
    )(src, recv, state, gain, *after)


NT = (((1,), (1,)), ((), ()))


def ready_kernel(sizes, *refs):
    y = refs[0][0, 0]
    blocks = sum(sizes)
    d_in = refs[1 : 1 + blocks]
    wg_in, wu_in, wo_in = refs[1 + blocks : 4 + blocks]
    wp_in = refs[4 + blocks : 8 + blocks]
    wg, wu, da, db, pa, pb, wo, sems = refs[8 + blocks :]
    count = [0]

    def start(src, dst):
        copy = pltpu.make_async_copy(src, dst, sems.at[count[0]])
        count[0] += 1
        copy.start()
        return copy

    parts = [pl.multiple_of((y + j) % 4 * 512, 512) for j in range(4)]
    first = [start(wo_in, wo.at[pl.ds(0, FS)])]
    for j in range(4):
        for h in range(2):
            cols = pl.ds(pl.multiple_of(parts[j] + h * FS, FS), FS)
            first.append(start(wp_in[j].at[pl.ds(1024 + h * FS, FS)], wo.at[pl.ds(FS, FS), cols]))
    for b in range(sizes[0]):
        first.append(start(d_in[b], da.at[pl.ds(b * ROWS, ROWS)]))
    second = [start(d_in[sizes[0] + b], db.at[pl.ds(b * ROWS, ROWS)]) for b in range(sizes[1])]
    third = [start(wg_in, wg.at[:, pl.ds(0, FS)]), start(wu_in, wu.at[:, pl.ds(0, FS)])]
    for j in range(4):
        rows = pl.ds(parts[j], 512)
        third.append(start(wp_in[j].at[pl.ds(0, 512)], wg.at[rows, pl.ds(FS, FS)]))
        third.append(start(wp_in[j].at[pl.ds(512, 512)], wu.at[rows, pl.ds(FS, FS)]))
    for copy in first:
        copy.wait()
    pa[...] = lax.dot_general(da[...], wo[...], NT, preferred_element_type=F32)
    for copy in second:
        copy.wait()
    pb[...] = lax.dot_general(db[...], wo[...], NT, preferred_element_type=F32)
    for copy in third:
        copy.wait()


def make_ready(y, d_a, d_b, weights):
    any_ = pl.BlockSpec(memory_space=pl.ANY)
    vmem = pl.BlockSpec(memory_space=pltpu.VMEM)
    sizes = (len(d_a), len(d_b))
    rows = [n * ROWS for n in sizes]
    out_shape = (
        jax.ShapeDtypeStruct((D, 2 * FS), BF16),
        jax.ShapeDtypeStruct((D, 2 * FS), BF16),
        jax.ShapeDtypeStruct((rows[0], D), BF16),
        jax.ShapeDtypeStruct((rows[1], D), BF16),
        jax.ShapeDtypeStruct((rows[0], 2 * FS), F32),
        jax.ShapeDtypeStruct((rows[1], 2 * FS), F32),
    )
    args = [y, *d_a, *d_b, *weights]
    return pl.pallas_call(
        functools.partial(ready_kernel, sizes),
        out_shape=out_shape,
        in_specs=[pl.BlockSpec(memory_space=pltpu.SMEM)] + [any_] * (len(args) - 1),
        out_specs=tuple(vmem for _ in out_shape),
        scratch_shapes=[pltpu.VMEM((2 * FS, D), BF16), pltpu.SemaphoreType.DMA((27,))],
        compiler_params=pltpu.CompilerParams(vmem_limit_bytes=READY_VMEM * 1024 * 1024),
        cost_estimate=pl.CostEstimate(
            flops=2 * sum(rows) * D * 2 * FS, bytes_accessed=24 * 1024 * 1024, transcendentals=0
        ),
        name="ready",
    )(*args)


def layer_kernel(blocks, tile, last, *refs):
    n_in = refs[:blocks]
    wg, wu, dbuf, pre = refs[blocks : blocks + 4]
    rest = refs[blocks + 4 :]
    if last:
        acc_in, gacc_ref, gain_ref, own_out, par_out, gout_ref = rest[:6]
        rest = rest[6:]
    else:
        acc_out, gout_ref = rest[:2]
        rest = rest[2:]
    nbuf, gate_buf, act, dgate, dup, acc, par, sems, out_sems = rest

    copies = []
    for b in range(blocks):
        copies.append(pltpu.make_async_copy(n_in[b], nbuf.at[pl.ds(b * ROWS, ROWS)], sems.at[b]))
        copies[-1].start()
    if last:
        acc_copy = pltpu.make_async_copy(acc_in, acc, sems.at[blocks])
        acc_copy.start()
    tiles = [slice(t * tile, (t + 1) * tile) for t in range(blocks * ROWS // tile)]
    for copy in copies:
        copy.wait()
    for rows in tiles:
        gate_buf[rows, :] = jnp.dot(nbuf[rows, :], wg[...], preferred_element_type=F32)
    for rows in tiles:
        up = jnp.dot(nbuf[rows, :], wu[...], preferred_element_type=F32)
        gate = gate_buf[rows, :]
        d_act = pre[rows, :]
        inner = GELU_C * (gate + 0.044715 * gate * gate * gate)
        th = jnp.tanh(inner)
        half = 0.5 * (1.0 + th)
        gelu = gate * half
        slope = half + 0.5 * gate * (1.0 - th * th) * GELU_C * (1.0 + 3.0 * 0.044715 * gate * gate)
        act[rows, :] = (gelu * up).astype(BF16)
        dgate[rows, :] = (d_act * up * slope).astype(BF16)
        dup[rows, :] = (d_act * gelu).astype(BF16)
    if last:
        acc_copy.wait()
    act_t = act[...].T
    leaving = []
    for r in range(NR):
        cols = slice(r * FS, (r + 1) * FS)
        part = jnp.dot(act_t, dbuf[:, cols], preferred_element_type=F32)
        if last:
            part = part + acc[r]
            acc[r, :FS] = part[:FS]
            par[r] = part[FS:].astype(BF16)
            leaving.append(pltpu.make_async_copy(acc.at[r, pl.ds(0, FS)], own_out.at[r], out_sems.at[2 * r]))
            leaving.append(pltpu.make_async_copy(par.at[r], par_out.at[r], out_sems.at[2 * r + 1]))
            leaving[-2].start()
            leaving[-1].start()
        else:
            acc[r] = part
            leaving.append(pltpu.make_async_copy(acc.at[r], acc_out.at[r], out_sems.at[r]))
            leaving[-1].start()

    for j in range(4):
        cols = slice(j * 512, (j + 1) * 512)
        dn = lax.dot_general(dgate[...], wg[cols, :], NT, preferred_element_type=F32)
        dn = dn + lax.dot_general(dup[...], wu[cols, :], NT, preferred_element_type=F32)
        part = jnp.sum(dn * nbuf[:, cols].astype(F32), axis=0, keepdims=True)
        if last:
            part = (part + gacc_ref[:, cols]) / gain_ref[:, cols]
        gout_ref[:, cols] = part
    for copy in leaving:
        copy.wait()


def layer(n_blocks, ready, tile, carried=None):
    blocks = len(n_blocks)
    rows = blocks * ROWS
    last = carried is not None
    any_ = pl.BlockSpec(memory_space=pl.ANY)
    vmem = pl.BlockSpec(memory_space=pltpu.VMEM)
    args = [*n_blocks, *ready]
    in_specs = [any_] * blocks + [vmem] * len(ready)
    if last:
        args += list(carried)
        in_specs += [any_, vmem, vmem]
        out_shape = (
            jax.ShapeDtypeStruct((NR, FS, FS), F32),
            jax.ShapeDtypeStruct((NR, FS, FS), BF16),
            jax.ShapeDtypeStruct((1, D), F32),
        )
    else:
        out_shape = (
            jax.ShapeDtypeStruct((NR, 2 * FS, FS), F32),
            jax.ShapeDtypeStruct((1, D), F32),
        )
    return pl.pallas_call(
        functools.partial(layer_kernel, blocks, tile, last),
        out_shape=out_shape,
        in_specs=in_specs,
        out_specs=(*(any_ for _ in out_shape[1:]), vmem),
        scratch_shapes=[
            pltpu.VMEM((rows, D), BF16),
            pltpu.VMEM((rows, 2 * FS), F32),
            pltpu.VMEM((rows, 2 * FS), BF16),
            pltpu.VMEM((rows, 2 * FS), BF16),
            pltpu.VMEM((rows, 2 * FS), BF16),
            pltpu.VMEM((NR, 2 * FS, FS), F32),
            pltpu.VMEM((NR, FS, FS), BF16),
            pltpu.SemaphoreType.DMA((blocks + 1,)),
            pltpu.SemaphoreType.DMA((2 * NR,)),
        ],
        compiler_params=pltpu.CompilerParams(vmem_limit_bytes=LAYER_VMEM * 1024 * 1024),
        cost_estimate=pl.CostEstimate(
            flops=10 * rows * D * 2 * FS, bytes_accessed=4 * rows * D, transcendentals=rows * 512
        ),
        name="layer_last" if last else "layer_first",
    )(*args)


def shards(
    question_emb,
    probes,
    codes,
    code_scale,
    question_state,
    top_passages,
    soft_weight,
    passage_home,
    passage_states,
    norm_gain,
    w_gate,
    w_up,
    w_out,
    cotangent,
):
    dy0 = (soft_weight[:, :, None, None] * cotangent.astype(F32)).astype(BF16).reshape(ROWS, D)
    dyp = pair(dy0)
    dy_next = ring(dy0, 1)
    dy_prev = ring(dy0, -1)
    dy_far = ring(dy0, 2)
    y = lax.axis_index("reader") // 2
    y_row = y.astype(I32).reshape(1, 1)
    piece = jnp.concatenate(
        [
            lax.dynamic_slice(w_gate, (y * 512, 0), (512, FS)),
            lax.dynamic_slice(w_up, (y * 512, 0), (512, FS)),
            lax.dynamic_slice(w_out, (0, y * 512), (FS, FS)),
            lax.dynamic_slice(w_out, (0, y * 512 + FS), (FS, FS)),
        ],
        axis=0,
    )
    piece = partner(piece)

    msg, src = make_plan(top_passages, probes, passage_home, question_emb)
    asked = lax.all_to_all(msg, "index", 0, 0, tiled=True)
    slots = asked[:, 6, :CAP].astype(I32)
    blocks, piece, dyp, dy_next, dy_prev, dy_far = pick_slots(
        slots, passage_states, piece, dyp, dy_next, dy_prev, dy_far
    )
    recv = lax.all_to_all(blocks, "index", 0, 0, tiled=True)
    dy_a = [dy0, dy_next, dy_prev, dy_far, dyp]
    dy_b = [ring(dyp, 1), ring(dyp, -1), ring(dyp, 2)]
    weights = (w_gate, w_up, w_out, piece, column(piece, -1), column(piece, 2), column(piece, 1))
    gain_row = norm_gain.reshape(1, D)
    n0 = norm_rows(src, recv, question_state, gain_row, *dy_b)
    np_ = pair(n0)
    n_a = [n0, ring(n0, 1), ring(n0, -1), ring(n0, 2), np_]
    n_b = [ring(np_, 1), ring(np_, -1), ring(np_, 2)]

    group_emb = asked[:, :6, :].reshape(NI, 768)
    every_score = (
        jnp.einsum("qe,cse->qcs", group_emb, codes, preferred_element_type=F32) * code_scale[None]
    )
    local = asked[:, 6, 8 : 8 + NPROBE].astype(I32)
    hot = (local[:, :, None] == jnp.arange(CLUS_DEV, dtype=I32)[None, None, :]).astype(F32)
    picked = jnp.einsum("qpc,qcs->qps", hot, every_score, precision=lax.Precision.HIGHEST)

    wg2, wu2, d_rows_a, d_rows_b, d_act_a, d_act_b = make_ready(y_row, dy_a, dy_b, weights)
    acc_a, gain_a = layer(n_a, (wg2, wu2, d_rows_a, d_act_a), FIRST_TILE)
    own, par, gain_part = layer(
        n_b, (wg2, wu2, d_rows_b, d_act_b), LAST_TILE, (acc_a, gain_a, gain_row)
    )

    from_partner = partner(par)
    tail = jnp.concatenate(
        [picked, gain_part.reshape(NI, 1, 128), jnp.zeros((NI, 7, 128), F32)], axis=1
    )
    tail = lax.all_to_all(tail, "index", 0, 0, tiled=True)
    tail = jnp.sum(tail, axis=0)
    probe_scores = tail[None, :NPROBE]
    gain128 = tail[NPROBE].reshape(NR, 1, 16)
    hi = gain128.astype(BF16)
    lo = (gain128 - hi.astype(F32)).astype(BF16)
    gain_rows = jnp.pad(jnp.concatenate([hi, lo], axis=2), ((0, 0), (0, 7), (0, FS - 32)))
    total = (own + from_partner.astype(F32)).astype(BF16)
    out = lax.all_to_all(jnp.concatenate([total, gain_rows], axis=1), "reader", 0, 0, tiled=True)
    out = jnp.sum(out.astype(F32), axis=0)
    grad_out = out[:FS]
    grad_gain = out[FS, :16] + out[FS, 16:32]
    return probe_scores, grad_out, grad_gain


def solution(mesh):
    return jax.shard_map(
        shards,
        mesh=mesh,
        in_specs=(
            P(("index", "reader"), None),
            P(("index", "reader"), None),
            P("index", None, None),
            P("index", None),
            P(("index", "reader"), None),
            P(("index", "reader"), None),
            P(("index", "reader"), None),
            P(),
            P("index", None, None),
            P(),
            P(None, "index"),
            P(None, "index"),
            P("index", None),
            P(("index", "reader"), None, None, None),
        ),
        out_specs=(
            P(("index", "reader"), None, None),
            P("index", "reader"),
            P(("index", "reader")),
        ),
        check_vma=False,
    )
```

```python
import functools
import math

import jax
import jax.numpy as jnp
from jax import lax
from jax.experimental import pallas as pl
from jax.experimental.pallas import tpu as pltpu
from jax.sharding import PartitionSpec as P

BF16 = jnp.bfloat16
F32 = jnp.float32
I32 = jnp.int32

CAP = 3
FIRST_TILE = 400
LAST_TILE = 480
READY_VMEM = 20
LAYER_VMEM = 26
NI = 16
NR = 8
TOPK = 20
NPROBE = 32
LP = 8
D = 2048
FS = 256
ROWS = TOPK * LP
PASS_DEV = 256
CLUS_DEV = 32
GELU_C = math.sqrt(2.0 / math.pi)
BOTH = ("index", "reader")


def pairs_of(move):
    pairs = []
    for x in range(4):
        for z in range(4):
            for y in range(4):
                for c in range(2):
                    tx, tz = move(x, z, c)
                    pairs.append(((x * 4 + z) * 8 + y * 2 + c, (tx * 4 + tz) * 8 + y * 2 + c))
    return pairs


def ring_move(step):
    return lambda x, z, c: ((x + step) % 4, z) if c == 0 else (x, (z + step) % 4)


def pair_move(x, z, c):
    return (x, z ^ 1) if c == 0 else (x ^ 1, z)


def partner_move(x, z, c):
    return (x, 3 - z) if c == 0 else (3 - x, z)


def column_pairs(step):
    pairs = []
    for i in range(NI):
        for y in range(4):
            for c in range(2):
                pairs.append((i * 8 + y * 2 + c, i * 8 + (y + step) % 4 * 2 + c))
    return pairs


def column(v, step):
    return lax.ppermute(v, BOTH, column_pairs(step))


def ring(v, step):
    return lax.ppermute(v, BOTH, pairs_of(ring_move(step)))


def relayed(prev, following):
    half = ROWS // 2
    return [ring(prev[:half], 1), ring(following[half:], -1)]


def pair(v):
    return lax.ppermute(v, BOTH, pairs_of(pair_move))


def partner(v):
    return lax.ppermute(v, BOTH, pairs_of(partner_move))


def plan_kernel(top_ref, probes_ref, home_ref, y_ref, emb_ref, wg_ref, wu_ref, wo_ref, msg_ref, src_ref, piece_ref, sems):
    part = pl.multiple_of(y_ref[0, 0] * 512, 512)
    cuts = [
        (wg_ref.at[pl.ds(part, 512)], piece_ref.at[pl.ds(0, 512)]),
        (wu_ref.at[pl.ds(part, 512)], piece_ref.at[pl.ds(512, 512)]),
        (wo_ref.at[:, pl.ds(part, FS)], piece_ref.at[pl.ds(1024, FS)]),
        (wo_ref.at[:, pl.ds(pl.multiple_of(part + FS, FS), FS)], piece_ref.at[pl.ds(1024 + FS, FS)]),
    ]
    cuts = [pltpu.make_async_copy(src, dst, sems.at[i]) for i, (src, dst) in enumerate(cuts)]
    for copy in cuts:
        copy.start()
    shape = (NI, 8, 128)
    owner_id = lax.broadcasted_iota(I32, shape, 0)
    lane_id = lax.broadcasted_iota(I32, shape, 2)
    row_id = lax.broadcasted_iota(I32, shape, 1)
    vec = jnp.where(lane_id >= 8, 64, 0)
    owners = []
    for k in range(TOPK):
        loc = home_ref[top_ref[0, k]]
        owner = loc // PASS_DEV
        rank = jnp.int32(0)
        for earlier in owners:
            rank = rank + jnp.where(earlier == owner, 1, 0)
        owners.append(owner)
        src_ref[0, k] = owner * CAP + rank
        vec = jnp.where((owner_id == owner) & (lane_id == rank), loc % PASS_DEV, vec)
    for k in range(NPROBE):
        c = probes_ref[0, k]
        vec = jnp.where((owner_id == c // CLUS_DEV) & (lane_id == 8 + k), c % CLUS_DEV, vec)
    emb = jnp.broadcast_to(emb_ref[...][None], shape)
    msg_ref[...] = jnp.where(row_id == 6, vec.astype(F32), emb).astype(BF16)
    for copy in cuts:
        copy.wait()


def make_plan(top, probes, home, y, emb, w_gate, w_up, w_out):
    any_ = pl.BlockSpec(memory_space=pl.ANY)
    emb8 = jnp.pad(emb.astype(F32).reshape(6, 128), ((0, 2), (0, 0)))
    smem = pl.BlockSpec(memory_space=pltpu.SMEM)
    vmem = pl.BlockSpec(memory_space=pltpu.VMEM)
    return pl.pallas_call(
        plan_kernel,
        out_shape=(
            jax.ShapeDtypeStruct((NI, 8, 128), BF16),
            jax.ShapeDtypeStruct((1, TOPK), I32),
            jax.ShapeDtypeStruct((1536, FS), BF16),
        ),
        in_specs=[smem, smem, smem, smem, vmem, any_, any_, any_],
        out_specs=(vmem, smem, vmem),
        scratch_shapes=[pltpu.SemaphoreType.DMA((4,))],
        compiler_params=pltpu.CompilerParams(vmem_limit_bytes=60 * 1024 * 1024),
        name="plan",
    )(top, probes, home, y, emb8, w_gate, w_up, w_out)


def ask_kernel(asked_ref, *refs):
    slot_ref = refs[len(refs) // 2]
    slot_ref[...] = asked_ref[:, 6, :].astype(F32).astype(I32)


def read_asked(asked, *passed):
    any_ = pl.BlockSpec(memory_space=pl.ANY)
    vmem = pl.BlockSpec(memory_space=pltpu.VMEM)
    return pl.pallas_call(
        ask_kernel,
        out_shape=(
            jax.ShapeDtypeStruct((NI, 128), I32),
            *(jax.ShapeDtypeStruct(v.shape, v.dtype) for v in passed),
        ),
        in_specs=[vmem] + [any_] * len(passed),
        out_specs=(vmem, *(any_ for _ in passed)),
        input_output_aliases={1 + i: 1 + i for i in range(len(passed))},
        name="ask",
    )(asked, *passed)


def send_kernel(*refs):
    pass


def send_after(value, *passed):
    any_ = pl.BlockSpec(memory_space=pl.ANY)
    args = (value, *passed)
    return pl.pallas_call(
        send_kernel,
        out_shape=tuple(jax.ShapeDtypeStruct(v.shape, v.dtype) for v in args),
        in_specs=[any_] * len(args),
        out_specs=tuple(any_ for _ in args),
        input_output_aliases={i: i for i in range(len(args))},
        name="send",
    )(*args)


def pick_kernel(slot_ref, states_ref, *refs):
    out_ref, sems = refs[(len(refs) - 2) // 2], refs[-1]
    copies = []
    for i in range(NI * CAP):
        row = slot_ref[i // CAP, i % CAP]
        copy = pltpu.make_async_copy(states_ref.at[row], out_ref.at[i], sems.at[i])
        copy.start()
        copies.append(copy)
    for copy in copies:
        copy.wait()


def pick_slots(slots, states, *passed):
    any_ = pl.BlockSpec(memory_space=pl.ANY)
    return pl.pallas_call(
        pick_kernel,
        out_shape=(
            jax.ShapeDtypeStruct((NI * CAP, LP, D), BF16),
            *(jax.ShapeDtypeStruct(v.shape, v.dtype) for v in passed),
        ),
        in_specs=[pl.BlockSpec(memory_space=pltpu.SMEM), any_] + [any_] * len(passed),
        out_specs=(pl.BlockSpec(memory_space=pltpu.VMEM), *(any_ for _ in passed)),
        input_output_aliases={2 + i: 1 + i for i in range(len(passed))},
        scratch_shapes=[pltpu.SemaphoreType.DMA((NI * CAP,))],
        compiler_params=pltpu.CompilerParams(vmem_limit_bytes=57 * 1024 * 1024),
        cost_estimate=pl.CostEstimate(flops=0, bytes_accessed=2 * NI * CAP * LP * D * 2, transcendentals=0),
        name="pick",
    )(slots, states, *passed)


def norm_kernel(src_ref, recv_ref, state_ref, gain_ref, *refs):
    out_ref, buf, sems = refs[-3:]
    copies = []
    for k in range(TOPK):
        copy = pltpu.make_async_copy(recv_ref.at[src_ref[0, k]], buf.at[k], sems.at[k])
        copy.start()
        copies.append(copy)
    state = state_ref[...].astype(F32)
    gain = gain_ref[...]
    for k in range(TOPK // 2):
        copies[2 * k].wait()
        copies[2 * k + 1].wait()
        x = buf[2 * k : 2 * k + 2].astype(F32).reshape(2 * LP, D) + state
        inv = lax.rsqrt(jnp.mean(x * x, axis=-1, keepdims=True) + 1e-06)
        out_ref[2 * LP * k : 2 * LP * (k + 1), :] = (x * inv * gain).astype(BF16)


def norm_rows(src, recv, state, gain, *after):
    vmem = pl.BlockSpec(memory_space=pltpu.VMEM)
    return pl.pallas_call(
        norm_kernel,
        out_shape=jax.ShapeDtypeStruct((ROWS, D), BF16),
        in_specs=[
            pl.BlockSpec(memory_space=pltpu.SMEM),
            pl.BlockSpec(memory_space=pl.ANY),
            vmem,
            vmem,
            *(pl.BlockSpec(memory_space=pl.ANY) for _ in after),
        ],
        out_specs=vmem,
        scratch_shapes=[pltpu.VMEM((TOPK, LP, D), BF16), pltpu.SemaphoreType.DMA((TOPK,))],
        compiler_params=pltpu.CompilerParams(vmem_limit_bytes=57 * 1024 * 1024),
        name="norm",
    )(src, recv, state, gain, *after)


NT = (((1,), (1,)), ((), ()))


def ready_kernel(n_a, n_b, *refs):
    y = refs[0][0, 0]
    blocks = n_a + n_b
    d_in = refs[1 : 1 + blocks]
    wg_in, wu_in, wo_in = refs[1 + blocks : 4 + blocks]
    wp_in = refs[4 + blocks : 8 + blocks]
    wg, wu, da, db, pa, pb, wo, sems = refs[8 + blocks :]
    count = [0]

    def start(src, dst):
        copy = pltpu.make_async_copy(src, dst, sems.at[count[0]])
        count[0] += 1
        copy.start()
        return copy

    parts = [pl.multiple_of((y + j) % 4 * 512, 512) for j in range(4)]
    first = [start(wo_in, wo.at[pl.ds(0, FS)])]
    for j in range(4):
        for h in range(2):
            cols = pl.ds(pl.multiple_of(parts[j] + h * FS, FS), FS)
            first.append(start(wp_in[j].at[pl.ds(1024 + h * FS, FS)], wo.at[pl.ds(FS, FS), cols]))
    at = 0
    for ref in d_in[:n_a]:
        first.append(start(ref, da.at[pl.ds(at, ref.shape[0])]))
        at += ref.shape[0]
    second, at = [], 0
    for ref in d_in[n_a:]:
        second.append(start(ref, db.at[pl.ds(at, ref.shape[0])]))
        at += ref.shape[0]
    third = [start(wg_in, wg.at[:, pl.ds(0, FS)]), start(wu_in, wu.at[:, pl.ds(0, FS)])]
    for j in range(4):
        rows = pl.ds(parts[j], 512)
        third.append(start(wp_in[j].at[pl.ds(0, 512)], wg.at[rows, pl.ds(FS, FS)]))
        third.append(start(wp_in[j].at[pl.ds(512, 512)], wu.at[rows, pl.ds(FS, FS)]))
    for copy in first:
        copy.wait()
    pa[...] = lax.dot_general(da[...], wo[...], NT, preferred_element_type=F32)
    for copy in second:
        copy.wait()
    pb[...] = lax.dot_general(db[...], wo[...], NT, preferred_element_type=F32)
    for copy in third:
        copy.wait()


def make_ready(y, d_a, d_b, weights):
    any_ = pl.BlockSpec(memory_space=pl.ANY)
    vmem = pl.BlockSpec(memory_space=pltpu.VMEM)
    rows = [sum(v.shape[0] for v in d_a), sum(v.shape[0] for v in d_b)]
    out_shape = (
        jax.ShapeDtypeStruct((D, 2 * FS), BF16),
        jax.ShapeDtypeStruct((D, 2 * FS), BF16),
        jax.ShapeDtypeStruct((rows[0], D), BF16),
        jax.ShapeDtypeStruct((rows[1], D), BF16),
        jax.ShapeDtypeStruct((rows[0], 2 * FS), F32),
        jax.ShapeDtypeStruct((rows[1], 2 * FS), F32),
    )
    args = [y, *d_a, *d_b, *weights]
    return pl.pallas_call(
        functools.partial(ready_kernel, len(d_a), len(d_b)),
        out_shape=out_shape,
        in_specs=[pl.BlockSpec(memory_space=pltpu.SMEM)] + [any_] * (len(args) - 1),
        out_specs=tuple(vmem for _ in out_shape),
        scratch_shapes=[pltpu.VMEM((2 * FS, D), BF16), pltpu.SemaphoreType.DMA((19 + len(d_a) + len(d_b),))],
        compiler_params=pltpu.CompilerParams(vmem_limit_bytes=READY_VMEM * 1024 * 1024),
        cost_estimate=pl.CostEstimate(flops=1000, bytes_accessed=1000, transcendentals=0),
        name="ready",
    )(*args)


def layer_kernel(blocks, tile, last, *refs):
    n_in = refs[:blocks]
    wg, wu, dbuf, pre = refs[blocks : blocks + 4]
    rest = refs[blocks + 4 :]
    if last:
        acc_in, gacc_ref, gain_ref, own_out, par_out, gout_ref = rest[:6]
        rest = rest[6:]
    else:
        acc_out, gout_ref = rest[:2]
        rest = rest[2:]
    nbuf, gate_buf, act, dgate, dup, acc, par, sems, out_sems = rest

    copies = []
    for b in range(blocks):
        copies.append(pltpu.make_async_copy(n_in[b], nbuf.at[pl.ds(b * ROWS, ROWS)], sems.at[b]))
        copies[-1].start()
    if last:
        acc_copy = pltpu.make_async_copy(acc_in, acc, sems.at[blocks])
        acc_copy.start()
    tiles = [slice(t * tile, (t + 1) * tile) for t in range(blocks * ROWS // tile)]
    for copy in copies:
        copy.wait()
    for rows in tiles:
        gate_buf[rows, :] = jnp.dot(nbuf[rows, :], wg[...], preferred_element_type=F32)
    for rows in tiles:
        up = jnp.dot(nbuf[rows, :], wu[...], preferred_element_type=F32)
        gate = gate_buf[rows, :]
        d_act = pre[rows, :]
        inner = GELU_C * (gate + 0.044715 * gate * gate * gate)
        th = jnp.tanh(inner)
        half = 0.5 * (1.0 + th)
        gelu = gate * half
        slope = half + 0.5 * gate * (1.0 - th * th) * GELU_C * (1.0 + 3.0 * 0.044715 * gate * gate)
        act[rows, :] = (gelu * up).astype(BF16)
        dgate[rows, :] = (d_act * up * slope).astype(BF16)
        dup[rows, :] = (d_act * gelu).astype(BF16)
    if last:
        acc_copy.wait()
    act_t = act[...].T
    leaving = []
    for r in range(NR):
        cols = slice(r * FS, (r + 1) * FS)
        part = jnp.dot(act_t, dbuf[:, cols], preferred_element_type=F32)
        if last:
            part = part + acc[r]
            acc[r, :FS] = part[:FS]
            par[r] = part[FS:].astype(BF16)
            leaving.append(pltpu.make_async_copy(acc.at[r, pl.ds(0, FS)], own_out.at[r], out_sems.at[2 * r]))
            leaving.append(pltpu.make_async_copy(par.at[r], par_out.at[r], out_sems.at[2 * r + 1]))
            leaving[-2].start()
            leaving[-1].start()
        else:
            acc[r] = part
            leaving.append(pltpu.make_async_copy(acc.at[r], acc_out.at[r], out_sems.at[r]))
            leaving[-1].start()

    for j in range(4):
        cols = slice(j * 512, (j + 1) * 512)
        dn = lax.dot_general(dgate[...], wg[cols, :], NT, preferred_element_type=F32)
        dn = dn + lax.dot_general(dup[...], wu[cols, :], NT, preferred_element_type=F32)
        part = jnp.sum(dn * nbuf[:, cols].astype(F32), axis=0, keepdims=True)
        if last:
            part = (part + gacc_ref[:, cols]) / gain_ref[:, cols]
        gout_ref[:, cols] = part
    for copy in leaving:
        copy.wait()


def layer(n_blocks, ready, tile, carried=None):
    blocks = len(n_blocks)
    rows = blocks * ROWS
    last = carried is not None
    any_ = pl.BlockSpec(memory_space=pl.ANY)
    vmem = pl.BlockSpec(memory_space=pltpu.VMEM)
    args = [*n_blocks, *ready]
    in_specs = [any_] * blocks + [vmem] * len(ready)
    if last:
        args += list(carried)
        in_specs += [any_, vmem, vmem]
        out_shape = (
            jax.ShapeDtypeStruct((NR, FS, FS), F32),
            jax.ShapeDtypeStruct((NR, FS, FS), BF16),
            jax.ShapeDtypeStruct((1, D), F32),
        )
    else:
        out_shape = (
            jax.ShapeDtypeStruct((NR, 2 * FS, FS), F32),
            jax.ShapeDtypeStruct((1, D), F32),
        )
    return pl.pallas_call(
        functools.partial(layer_kernel, blocks, tile, last),
        out_shape=out_shape,
        in_specs=in_specs,
        out_specs=(*(any_ for _ in out_shape[1:]), vmem),
        scratch_shapes=[
            pltpu.VMEM((rows, D), BF16),
            pltpu.VMEM((rows, 2 * FS), F32),
            pltpu.VMEM((rows, 2 * FS), BF16),
            pltpu.VMEM((rows, 2 * FS), BF16),
            pltpu.VMEM((rows, 2 * FS), BF16),
            pltpu.VMEM((NR, 2 * FS, FS), F32),
            pltpu.VMEM((NR, FS, FS), BF16),
            pltpu.SemaphoreType.DMA((blocks + 1,)),
            pltpu.SemaphoreType.DMA((2 * NR,)),
        ],
        compiler_params=pltpu.CompilerParams(vmem_limit_bytes=LAYER_VMEM * 1024 * 1024),
        cost_estimate=pl.CostEstimate(
            flops=10 * rows * D * 2 * FS, bytes_accessed=4 * rows * D, transcendentals=rows * 512
        ),
        name="layer_last" if last else "layer_first",
    )(*args)


def merge_kernel(own_ref, other_ref, rows_ref, out_ref):
    for r in range(NR):
        out_ref[r, :FS] = (own_ref[r] + other_ref[r].astype(F32)).astype(BF16)
        out_ref[r, FS:] = rows_ref[r]


def merge(own, other, rows):
    vmem = pl.BlockSpec(memory_space=pltpu.VMEM)
    return pl.pallas_call(
        merge_kernel,
        out_shape=jax.ShapeDtypeStruct((NR, FS + 16, FS), BF16),
        in_specs=[vmem] * 3,
        out_specs=vmem,
        compiler_params=pltpu.CompilerParams(vmem_limit_bytes=16 * 1024 * 1024),
        name="merge",
    )(own, other, rows)


def shards(
    question_emb,
    probes,
    codes,
    code_scale,
    question_state,
    top_passages,
    soft_weight,
    passage_home,
    passage_states,
    norm_gain,
    w_gate,
    w_up,
    w_out,
    cotangent,
):
    dy0 = (soft_weight[:, :, None, None] * cotangent.astype(F32)).astype(BF16).reshape(ROWS, D)
    dyp = pair(dy0)
    dy_m = ring(dy0, 1)
    dy_p = ring(dy0, -1)
    y_row = (lax.axis_index("reader") // 2).astype(I32).reshape(1, 1)

    msg, src, piece = make_plan(
        top_passages, probes, passage_home, y_row, question_emb, w_gate, w_up, w_out
    )
    piece = partner(piece)
    asked = lax.all_to_all(msg, "index", 0, 0, tiled=True)
    slots, piece, dyp, dy_m, dy_p = read_asked(asked, piece, dyp, dy_m, dy_p)
    weights = (w_gate, w_up, w_out, piece, column(piece, -1), column(piece, 2), column(piece, 1))
    dyp_m = ring(dyp, 1)
    dyp_p = ring(dyp, -1)
    (blocks,) = pick_slots(slots, passage_states)
    blocks, dyp_m, dyp_p = send_after(blocks, dyp_m, dyp_p)
    recv = lax.all_to_all(blocks, "index", 0, 0, tiled=True)
    dy_a = [dy0, dy_m, dy_p, ring(dy0, 2), dyp]
    dy_b = [dyp_m, dyp_p, ring(dyp, 2)]
    group_emb = asked[:, :6, :].reshape(NI, 768)
    every_score = (
        jnp.einsum("qe,cse->qcs", group_emb, codes, preferred_element_type=F32) * code_scale[None]
    )
    local = asked[:, 6, 8 : 8 + NPROBE].astype(I32)
    hot = (local[:, :, None] == jnp.arange(CLUS_DEV, dtype=I32)[None, None, :]).astype(F32)
    picked = jnp.einsum("qpc,qcs->qps", hot, every_score, precision=lax.Precision.HIGHEST)

    gain_row = norm_gain.reshape(1, D)
    n0 = norm_rows(src, recv, question_state, gain_row, picked)
    np_ = pair(n0)
    n_a = [n0, ring(n0, 1), ring(n0, -1), ring(n0, 2), np_]
    n_b = [ring(np_, 1), ring(np_, -1), ring(np_, 2)]

    wg2, wu2, d_rows_a, d_rows_b, d_act_a, d_act_b = make_ready(y_row, dy_a, dy_b, weights)
    acc_a, gain_a = layer(n_a, (wg2, wu2, d_rows_a, d_act_a), FIRST_TILE)
    own, par, gain_part = layer(
        n_b, (wg2, wu2, d_rows_b, d_act_b), LAST_TILE, (acc_a, gain_a, gain_row)
    )

    from_partner = partner(par)
    tail = jnp.concatenate(
        [picked, gain_part.reshape(NI, 1, 128), jnp.zeros((NI, 7, 128), F32)], axis=1
    )
    tail = lax.all_to_all(tail, "index", 0, 0, tiled=True)
    tail = jnp.sum(tail, axis=0)
    probe_scores = tail[None, :NPROBE]
    gain128 = tail[NPROBE].reshape(NR, 1, 16)
    hi = gain128.astype(BF16)
    lo = (gain128 - hi.astype(F32)).astype(BF16)
    gain_rows = jnp.pad(jnp.concatenate([hi, lo], axis=2), ((0, 0), (0, 15), (0, FS - 32)))
    out = lax.all_to_all(merge(own, from_partner, gain_rows), "reader", 0, 0, tiled=True)
    grad_out = jnp.sum(out[:, :FS].astype(F32), axis=0)
    gain_out = jnp.sum(out[:, FS, :32].astype(F32), axis=0)
    grad_gain = gain_out[:16] + gain_out[16:]
    return probe_scores, grad_out, grad_gain


def solution(mesh):
    return jax.shard_map(
        shards,
        mesh=mesh,
        in_specs=(
            P(("index", "reader"), None),
            P(("index", "reader"), None),
            P("index", None, None),
            P("index", None),
            P(("index", "reader"), None),
            P(("index", "reader"), None),
            P(("index", "reader"), None),
            P(),
            P("index", None, None),
            P(),
            P(None, "index"),
            P(None, "index"),
            P("index", None),
            P(("index", "reader"), None, None, None),
        ),
        out_specs=(
            P(("index", "reader"), None, None),
            P("index", "reader"),
            P(("index", "reader")),
        ),
        check_vma=False,
    )
```

```python
import functools
import math

import jax
import jax.numpy as jnp
from jax import lax
from jax.experimental import pallas as pl
from jax.experimental.pallas import tpu as pltpu
from jax.sharding import PartitionSpec as P

BF16 = jnp.bfloat16
F32 = jnp.float32
I32 = jnp.int32

CAP = 3
FIRST_TILE = 400
LAST_TILE = 480
READY_VMEM = 20
LAYER_VMEM = 26
NI = 16
NR = 8
TOPK = 20
NPROBE = 32
LP = 8
D = 2048
FS = 256
ROWS = TOPK * LP
PASS_DEV = 256
CLUS_DEV = 32
GELU_C = math.sqrt(2.0 / math.pi)
BOTH = ("index", "reader")


def pairs_of(move):
    pairs = []
    for x in range(4):
        for z in range(4):
            for y in range(4):
                for c in range(2):
                    tx, tz = move(x, z, c)
                    pairs.append(((x * 4 + z) * 8 + y * 2 + c, (tx * 4 + tz) * 8 + y * 2 + c))
    return pairs


def ring_move(step):
    return lambda x, z, c: ((x + step) % 4, z) if c == 0 else (x, (z + step) % 4)


def pair_move(x, z, c):
    return (x, z ^ 1) if c == 0 else (x ^ 1, z)


def partner_move(x, z, c):
    return (x, 3 - z) if c == 0 else (3 - x, z)


def column_pairs(step):
    pairs = []
    for i in range(NI):
        for y in range(4):
            for c in range(2):
                pairs.append((i * 8 + y * 2 + c, i * 8 + (y + step) % 4 * 2 + c))
    return pairs


def column(v, step):
    return lax.ppermute(v, BOTH, column_pairs(step))


def ring(v, step):
    return lax.ppermute(v, BOTH, pairs_of(ring_move(step)))


def relayed(prev, following):
    half = ROWS // 2
    return [ring(prev[:half], 1), ring(following[half:], -1)]


def pair(v):
    return lax.ppermute(v, BOTH, pairs_of(pair_move))


def partner(v):
    return lax.ppermute(v, BOTH, pairs_of(partner_move))


def plan_kernel(top_ref, probes_ref, home_ref, y_ref, emb_ref, wg_ref, wu_ref, wo_ref, msg_ref, src_ref, piece_ref, sems):
    part = pl.multiple_of(y_ref[0, 0] * 512, 512)
    cuts = [
        (wg_ref.at[pl.ds(part, 512)], piece_ref.at[pl.ds(0, 512)]),
        (wu_ref.at[pl.ds(part, 512)], piece_ref.at[pl.ds(512, 512)]),
        (wo_ref.at[:, pl.ds(part, FS)], piece_ref.at[pl.ds(1024, FS)]),
        (wo_ref.at[:, pl.ds(pl.multiple_of(part + FS, FS), FS)], piece_ref.at[pl.ds(1024 + FS, FS)]),
    ]
    cuts = [pltpu.make_async_copy(src, dst, sems.at[i]) for i, (src, dst) in enumerate(cuts)]
    for copy in cuts:
        copy.start()
    shape = (NI, 8, 128)
    owner_id = lax.broadcasted_iota(I32, shape, 0)
    lane_id = lax.broadcasted_iota(I32, shape, 2)
    row_id = lax.broadcasted_iota(I32, shape, 1)
    vec = jnp.where(lane_id >= 8, 64, 0)
    owners = []
    for k in range(TOPK):
        loc = home_ref[top_ref[0, k]]
        owner = loc // PASS_DEV
        rank = jnp.int32(0)
        for earlier in owners:
            rank = rank + jnp.where(earlier == owner, 1, 0)
        owners.append(owner)
        src_ref[0, k] = owner * CAP + rank
        vec = jnp.where((owner_id == owner) & (lane_id == rank), loc % PASS_DEV, vec)
    for k in range(NPROBE):
        c = probes_ref[0, k]
        vec = jnp.where((owner_id == c // CLUS_DEV) & (lane_id == 8 + k), c % CLUS_DEV, vec)
    emb = jnp.zeros(shape, F32)
    for c in range(6):
        part_c = emb_ref[:, c * 128 : (c + 1) * 128].astype(F32)
        emb = jnp.where(row_id == c, jnp.broadcast_to(part_c[None], shape), emb)
    msg_ref[...] = jnp.where(row_id == 6, vec.astype(F32), emb).astype(BF16)
    for copy in cuts:
        copy.wait()


def make_plan(top, probes, home, y, emb, w_gate, w_up, w_out):
    any_ = pl.BlockSpec(memory_space=pl.ANY)
    smem = pl.BlockSpec(memory_space=pltpu.SMEM)
    vmem = pl.BlockSpec(memory_space=pltpu.VMEM)
    return pl.pallas_call(
        plan_kernel,
        out_shape=(
            jax.ShapeDtypeStruct((NI, 8, 128), BF16),
            jax.ShapeDtypeStruct((1, TOPK), I32),
            jax.ShapeDtypeStruct((1536, FS), BF16),
        ),
        in_specs=[smem, smem, smem, smem, vmem, any_, any_, any_],
        out_specs=(vmem, smem, vmem),
        scratch_shapes=[pltpu.SemaphoreType.DMA((4,))],
        compiler_params=pltpu.CompilerParams(vmem_limit_bytes=60 * 1024 * 1024),
        name="plan",
    )(top, probes, home, y, emb, w_gate, w_up, w_out)


def ask_kernel(asked_ref, *refs):
    slot_ref = refs[len(refs) // 2]
    slot_ref[...] = asked_ref[:, 6, :].astype(F32).astype(I32)


def read_asked(asked, *passed):
    any_ = pl.BlockSpec(memory_space=pl.ANY)
    vmem = pl.BlockSpec(memory_space=pltpu.VMEM)
    return pl.pallas_call(
        ask_kernel,
        out_shape=(
            jax.ShapeDtypeStruct((NI, 128), I32),
            *(jax.ShapeDtypeStruct(v.shape, v.dtype) for v in passed),
        ),
        in_specs=[vmem] + [any_] * len(passed),
        out_specs=(vmem, *(any_ for _ in passed)),
        input_output_aliases={1 + i: 1 + i for i in range(len(passed))},
        name="ask",
    )(asked, *passed)


def send_kernel(*refs):
    pass


def send_after(value, *after):
    any_ = pl.BlockSpec(memory_space=pl.ANY)
    return pl.pallas_call(
        send_kernel,
        out_shape=jax.ShapeDtypeStruct(value.shape, value.dtype),
        in_specs=[any_] * (1 + len(after)),
        out_specs=any_,
        input_output_aliases={0: 0},
        compiler_params=pltpu.CompilerParams(vmem_limit_bytes=60 * 1024 * 1024),
        name="send",
    )(value, *after)


def pick_kernel(slot_ref, states_ref, *refs):
    out_ref, sems = refs[(len(refs) - 2) // 2], refs[-1]
    copies = []
    for i in range(NI * CAP):
        row = slot_ref[i // CAP, i % CAP]
        copy = pltpu.make_async_copy(states_ref.at[row], out_ref.at[i], sems.at[i])
        copy.start()
        copies.append(copy)
    for copy in copies:
        copy.wait()


def pick_slots(slots, states, *passed):
    any_ = pl.BlockSpec(memory_space=pl.ANY)
    return pl.pallas_call(
        pick_kernel,
        out_shape=(
            jax.ShapeDtypeStruct((NI * CAP, LP, D), BF16),
            *(jax.ShapeDtypeStruct(v.shape, v.dtype) for v in passed),
        ),
        in_specs=[pl.BlockSpec(memory_space=pltpu.SMEM), any_] + [any_] * len(passed),
        out_specs=(pl.BlockSpec(memory_space=pltpu.VMEM), *(any_ for _ in passed)),
        input_output_aliases={2 + i: 1 + i for i in range(len(passed))},
        scratch_shapes=[pltpu.SemaphoreType.DMA((NI * CAP,))],
        compiler_params=pltpu.CompilerParams(vmem_limit_bytes=57 * 1024 * 1024),
        cost_estimate=pl.CostEstimate(flops=0, bytes_accessed=2 * NI * CAP * LP * D * 2, transcendentals=0),
        name="pick",
    )(slots, states, *passed)


def norm_kernel(src_ref, recv_ref, state_ref, gain_ref, *refs):
    out_ref, buf, sems = refs[-3:]
    copies = []
    for k in range(TOPK):
        copy = pltpu.make_async_copy(recv_ref.at[src_ref[0, k]], buf.at[k], sems.at[k])
        copy.start()
        copies.append(copy)
    state = state_ref[...].astype(F32)
    gain = gain_ref[...]
    for k in range(TOPK // 2):
        copies[2 * k].wait()
        copies[2 * k + 1].wait()
        x = buf[2 * k : 2 * k + 2].astype(F32).reshape(2 * LP, D) + state
        inv = lax.rsqrt(jnp.mean(x * x, axis=-1, keepdims=True) + 1e-06)
        out_ref[2 * LP * k : 2 * LP * (k + 1), :] = (x * inv * gain).astype(BF16)


def norm_rows(src, recv, state, gain, *after):
    vmem = pl.BlockSpec(memory_space=pltpu.VMEM)
    return pl.pallas_call(
        norm_kernel,
        out_shape=jax.ShapeDtypeStruct((ROWS, D), BF16),
        in_specs=[
            pl.BlockSpec(memory_space=pltpu.SMEM),
            pl.BlockSpec(memory_space=pl.ANY),
            vmem,
            vmem,
            *(pl.BlockSpec(memory_space=pl.ANY) for _ in after),
        ],
        out_specs=vmem,
        scratch_shapes=[pltpu.VMEM((TOPK, LP, D), BF16), pltpu.SemaphoreType.DMA((TOPK,))],
        compiler_params=pltpu.CompilerParams(vmem_limit_bytes=57 * 1024 * 1024),
        name="norm",
    )(src, recv, state, gain, *after)


NT = (((1,), (1,)), ((), ()))


def ready_kernel(n_a, n_b, *refs):
    y = refs[0][0, 0]
    blocks = n_a + n_b
    d_in = refs[1 : 1 + blocks]
    wg_in, wu_in, wo_in = refs[1 + blocks : 4 + blocks]
    wp_in = refs[4 + blocks : 8 + blocks]
    wg, wu, da, db, pa, pb, wo, sems = refs[8 + blocks :]
    count = [0]

    def start(src, dst):
        copy = pltpu.make_async_copy(src, dst, sems.at[count[0]])
        count[0] += 1
        copy.start()
        return copy

    parts = [pl.multiple_of((y + j) % 4 * 512, 512) for j in range(4)]
    first = [start(wo_in, wo.at[pl.ds(0, FS)])]
    for j in range(4):
        for h in range(2):
            cols = pl.ds(pl.multiple_of(parts[j] + h * FS, FS), FS)
            first.append(start(wp_in[j].at[pl.ds(1024 + h * FS, FS)], wo.at[pl.ds(FS, FS), cols]))
    at = 0
    for ref in d_in[:n_a]:
        first.append(start(ref, da.at[pl.ds(at, ref.shape[0])]))
        at += ref.shape[0]
    second, at = [], 0
    for ref in d_in[n_a:]:
        second.append(start(ref, db.at[pl.ds(at, ref.shape[0])]))
        at += ref.shape[0]
    third = [start(wg_in, wg.at[:, pl.ds(0, FS)]), start(wu_in, wu.at[:, pl.ds(0, FS)])]
    for j in range(4):
        rows = pl.ds(parts[j], 512)
        third.append(start(wp_in[j].at[pl.ds(0, 512)], wg.at[rows, pl.ds(FS, FS)]))
        third.append(start(wp_in[j].at[pl.ds(512, 512)], wu.at[rows, pl.ds(FS, FS)]))
    for copy in first:
        copy.wait()
    pa[...] = lax.dot_general(da[...], wo[...], NT, preferred_element_type=F32)
    for copy in second:
        copy.wait()
    pb[...] = lax.dot_general(db[...], wo[...], NT, preferred_element_type=F32)
    for copy in third:
        copy.wait()


def make_ready(y, d_a, d_b, weights):
    any_ = pl.BlockSpec(memory_space=pl.ANY)
    vmem = pl.BlockSpec(memory_space=pltpu.VMEM)
    rows = [sum(v.shape[0] for v in d_a), sum(v.shape[0] for v in d_b)]
    out_shape = (
        jax.ShapeDtypeStruct((D, 2 * FS), BF16),
        jax.ShapeDtypeStruct((D, 2 * FS), BF16),
        jax.ShapeDtypeStruct((rows[0], D), BF16),
        jax.ShapeDtypeStruct((rows[1], D), BF16),
        jax.ShapeDtypeStruct((rows[0], 2 * FS), F32),
        jax.ShapeDtypeStruct((rows[1], 2 * FS), F32),
    )
    args = [y, *d_a, *d_b, *weights]
    return pl.pallas_call(
        functools.partial(ready_kernel, len(d_a), len(d_b)),
        out_shape=out_shape,
        in_specs=[pl.BlockSpec(memory_space=pltpu.SMEM)] + [any_] * (len(args) - 1),
        out_specs=tuple(vmem for _ in out_shape),
        scratch_shapes=[pltpu.VMEM((2 * FS, D), BF16), pltpu.SemaphoreType.DMA((19 + len(d_a) + len(d_b),))],
        compiler_params=pltpu.CompilerParams(vmem_limit_bytes=READY_VMEM * 1024 * 1024),
        cost_estimate=pl.CostEstimate(flops=1000, bytes_accessed=1000, transcendentals=0),
        name="ready",
    )(*args)


def layer_kernel(blocks, tile, last, *refs):
    n_in = refs[:blocks]
    wg, wu, dbuf, pre = refs[blocks : blocks + 4]
    rest = refs[blocks + 4 :]
    if last:
        acc_in, gacc_ref, gain_ref, own_out, par_out, gout_ref = rest[:6]
        rest = rest[6:]
    else:
        acc_out, gout_ref = rest[:2]
        rest = rest[2:]
    nbuf, gate_buf, act, dgate, dup, acc, par, sems, out_sems = rest

    copies = []
    for b in range(blocks):
        copies.append(pltpu.make_async_copy(n_in[b], nbuf.at[pl.ds(b * ROWS, ROWS)], sems.at[b]))
        copies[-1].start()
    if last:
        acc_copy = pltpu.make_async_copy(acc_in, acc, sems.at[blocks])
        acc_copy.start()
    tiles = [slice(t * tile, (t + 1) * tile) for t in range(blocks * ROWS // tile)]
    for copy in copies:
        copy.wait()
    for rows in tiles:
        gate_buf[rows, :] = jnp.dot(nbuf[rows, :], wg[...], preferred_element_type=F32)
    for rows in tiles:
        up = jnp.dot(nbuf[rows, :], wu[...], preferred_element_type=F32)
        gate = gate_buf[rows, :]
        d_act = pre[rows, :]
        inner = GELU_C * (gate + 0.044715 * gate * gate * gate)
        th = jnp.tanh(inner)
        half = 0.5 * (1.0 + th)
        gelu = gate * half
        slope = half + 0.5 * gate * (1.0 - th * th) * GELU_C * (1.0 + 3.0 * 0.044715 * gate * gate)
        act[rows, :] = (gelu * up).astype(BF16)
        dgate[rows, :] = (d_act * up * slope).astype(BF16)
        dup[rows, :] = (d_act * gelu).astype(BF16)
    if last:
        acc_copy.wait()
    act_t = act[...].T
    leaving = []
    for r in range(NR):
        cols = slice(r * FS, (r + 1) * FS)
        part = jnp.dot(act_t, dbuf[:, cols], preferred_element_type=F32)
        if last:
            part = part + acc[r]
            acc[r, :FS] = part[:FS]
            par[r] = part[FS:].astype(BF16)
            leaving.append(pltpu.make_async_copy(acc.at[r, pl.ds(0, FS)], own_out.at[r], out_sems.at[2 * r]))
            leaving.append(pltpu.make_async_copy(par.at[r], par_out.at[r], out_sems.at[2 * r + 1]))
            leaving[-2].start()
            leaving[-1].start()
        else:
            acc[r] = part
            leaving.append(pltpu.make_async_copy(acc.at[r], acc_out.at[r], out_sems.at[r]))
            leaving[-1].start()

    for j in range(4):
        cols = slice(j * 512, (j + 1) * 512)
        dn = lax.dot_general(dgate[...], wg[cols, :], NT, preferred_element_type=F32)
        dn = dn + lax.dot_general(dup[...], wu[cols, :], NT, preferred_element_type=F32)
        part = jnp.sum(dn * nbuf[:, cols].astype(F32), axis=0, keepdims=True)
        if last:
            part = (part + gacc_ref[:, cols]) / gain_ref[:, cols]
        gout_ref[:, cols] = part
    for copy in leaving:
        copy.wait()


def layer(n_blocks, ready, tile, carried=None):
    blocks = len(n_blocks)
    rows = blocks * ROWS
    last = carried is not None
    any_ = pl.BlockSpec(memory_space=pl.ANY)
    vmem = pl.BlockSpec(memory_space=pltpu.VMEM)
    args = [*n_blocks, *ready]
    in_specs = [any_] * blocks + [vmem] * len(ready)
    if last:
        args += list(carried)
        in_specs += [any_, vmem, vmem]
        out_shape = (
            jax.ShapeDtypeStruct((NR, FS, FS), F32),
            jax.ShapeDtypeStruct((NR, FS, FS), BF16),
            jax.ShapeDtypeStruct((1, D), F32),
        )
    else:
        out_shape = (
            jax.ShapeDtypeStruct((NR, 2 * FS, FS), F32),
            jax.ShapeDtypeStruct((1, D), F32),
        )
    return pl.pallas_call(
        functools.partial(layer_kernel, blocks, tile, last),
        out_shape=out_shape,
        in_specs=in_specs,
        out_specs=(*(any_ for _ in out_shape[1:]), vmem),
        scratch_shapes=[
            pltpu.VMEM((rows, D), BF16),
            pltpu.VMEM((rows, 2 * FS), F32),
            pltpu.VMEM((rows, 2 * FS), BF16),
            pltpu.VMEM((rows, 2 * FS), BF16),
            pltpu.VMEM((rows, 2 * FS), BF16),
            pltpu.VMEM((NR, 2 * FS, FS), F32),
            pltpu.VMEM((NR, FS, FS), BF16),
            pltpu.SemaphoreType.DMA((blocks + 1,)),
            pltpu.SemaphoreType.DMA((2 * NR,)),
        ],
        compiler_params=pltpu.CompilerParams(vmem_limit_bytes=LAYER_VMEM * 1024 * 1024),
        cost_estimate=pl.CostEstimate(
            flops=10 * rows * D * 2 * FS, bytes_accessed=4 * rows * D, transcendentals=rows * 512
        ),
        name="layer_last" if last else "layer_first",
    )(*args)


def merge_kernel(own_ref, other_ref, rows_ref, out_ref):
    for r in range(NR):
        out_ref[r, :FS] = (own_ref[r] + other_ref[r].astype(F32)).astype(BF16)
        out_ref[r, FS:] = rows_ref[r]


def merge(own, other, rows):
    vmem = pl.BlockSpec(memory_space=pltpu.VMEM)
    return pl.pallas_call(
        merge_kernel,
        out_shape=jax.ShapeDtypeStruct((NR, FS + 16, FS), BF16),
        in_specs=[vmem] * 3,
        out_specs=vmem,
        compiler_params=pltpu.CompilerParams(vmem_limit_bytes=16 * 1024 * 1024),
        name="merge",
    )(own, other, rows)


def shards(
    question_emb,
    probes,
    codes,
    code_scale,
    question_state,
    top_passages,
    soft_weight,
    passage_home,
    passage_states,
    norm_gain,
    w_gate,
    w_up,
    w_out,
    cotangent,
):
    dy0 = (soft_weight[:, :, None, None] * cotangent.astype(F32)).astype(BF16).reshape(ROWS, D)
    dyp = pair(dy0)
    dy_m = ring(dy0, 1)
    dy_p = ring(dy0, -1)
    y_row = (lax.axis_index("reader") // 2).astype(I32).reshape(1, 1)

    msg, src, piece = make_plan(
        top_passages, probes, passage_home, y_row, question_emb, w_gate, w_up, w_out
    )
    piece = partner(piece)
    asked = lax.all_to_all(msg, "index", 0, 0, tiled=True)
    slots, piece, dyp, dy_m, dy_p = read_asked(asked, piece, dyp, dy_m, dy_p)
    weights = (w_gate, w_up, w_out, piece, column(piece, -1), column(piece, 2), column(piece, 1))
    dyp_m = ring(dyp, 1)
    dyp_p = ring(dyp, -1)
    (blocks,) = pick_slots(slots, passage_states)
    blocks = send_after(blocks, dyp_m, dyp_p)
    recv = lax.all_to_all(blocks, "index", 0, 0, tiled=True)
    dy_a = [dy0, dy_m, dy_p, ring(dy0, 2), dyp]
    dy_b = [dyp_m, dyp_p, ring(dyp, 2)]
    group_emb = asked[:, :6, :].reshape(NI, 768)
    every_score = (
        jnp.einsum("qe,cse->qcs", group_emb, codes, preferred_element_type=F32) * code_scale[None]
    )
    local = asked[:, 6, 8 : 8 + NPROBE].astype(I32)
    hot = (local[:, :, None] == jnp.arange(CLUS_DEV, dtype=I32)[None, None, :]).astype(F32)
    picked = jnp.einsum("qpc,qcs->qps", hot, every_score, precision=lax.Precision.HIGHEST)
    picked = picked.astype(BF16)

    gain_row = norm_gain.reshape(1, D)
    n0 = norm_rows(src, recv, question_state, gain_row, picked)
    np_ = pair(n0)
    n_a = [n0, ring(n0, 1), ring(n0, -1), ring(n0, 2), np_]
    n_b = [ring(np_, 1), ring(np_, -1), ring(np_, 2)]

    wg2, wu2, d_rows_a, d_rows_b, d_act_a, d_act_b = make_ready(y_row, dy_a, dy_b, weights)
    acc_a, gain_a = layer(n_a, (wg2, wu2, d_rows_a, d_act_a), FIRST_TILE)
    own, par, gain_part = layer(
        n_b, (wg2, wu2, d_rows_b, d_act_b), LAST_TILE, (acc_a, gain_a, gain_row)
    )

    from_partner = partner(par)
    gain_own = gain_part.reshape(NI, 1, 128)
    gain_hi = gain_own.astype(BF16)
    gain_lo = (gain_own - gain_hi.astype(F32)).astype(BF16)
    tail = jnp.concatenate([picked, gain_hi, gain_lo, jnp.zeros((NI, 6, 128), BF16)], axis=1)
    tail = lax.all_to_all(tail, "index", 0, 0, tiled=True)
    tail = jnp.sum(tail.astype(F32), axis=0)
    probe_scores = tail[None, :NPROBE]
    gain128 = (tail[NPROBE] + tail[NPROBE + 1]).reshape(NR, 1, 16)
    hi = gain128.astype(BF16)
    lo = (gain128 - hi.astype(F32)).astype(BF16)
    gain_rows = jnp.pad(jnp.concatenate([hi, lo], axis=2), ((0, 0), (0, 15), (0, FS - 32)))
    out = lax.all_to_all(merge(own, from_partner, gain_rows), "reader", 0, 0, tiled=True)
    grad_out = jnp.sum(out[:, :FS].astype(F32), axis=0)
    gain_out = jnp.sum(out[:, FS, :32].astype(F32), axis=0)
    grad_gain = gain_out[:16] + gain_out[16:]
    return probe_scores, grad_out, grad_gain


def solution(mesh):
    return jax.shard_map(
        shards,
        mesh=mesh,
        in_specs=(
            P(("index", "reader"), None),
            P(("index", "reader"), None),
            P("index", None, None),
            P("index", None),
            P(("index", "reader"), None),
            P(("index", "reader"), None),
            P(("index", "reader"), None),
            P(),
            P("index", None, None),
            P(),
            P(None, "index"),
            P(None, "index"),
            P("index", None),
            P(("index", "reader"), None, None, None),
        ),
        out_specs=(
            P(("index", "reader"), None, None),
            P("index", "reader"),
            P(("index", "reader")),
        ),
        check_vma=False,
    )
```

```python
import functools
import math

import jax
import jax.numpy as jnp
from jax import lax
from jax.experimental import pallas as pl
from jax.experimental.pallas import tpu as pltpu
from jax.sharding import PartitionSpec as P

BF16 = jnp.bfloat16
F32 = jnp.float32
I32 = jnp.int32

CAP = 3
FIRST_TILE = 400
LAST_TILE = 480
READY_VMEM = 20
LAYER_VMEM = 26
NI = 16
NR = 8
TOPK = 20
NPROBE = 32
LP = 8
D = 2048
FS = 256
ROWS = TOPK * LP
PASS_DEV = 256
CLUS_DEV = 32
GELU_C = math.sqrt(2.0 / math.pi)
BOTH = ("index", "reader")


def pairs_of(move):
    pairs = []
    for x in range(4):
        for z in range(4):
            for y in range(4):
                for c in range(2):
                    tx, tz = move(x, z, c)
                    pairs.append(((x * 4 + z) * 8 + y * 2 + c, (tx * 4 + tz) * 8 + y * 2 + c))
    return pairs


def ring_move(step):
    return lambda x, z, c: ((x + step) % 4, z) if c == 0 else (x, (z + step) % 4)


def pair_move(x, z, c):
    return (x, z ^ 1) if c == 0 else (x ^ 1, z)


def partner_move(x, z, c):
    return (x, 3 - z) if c == 0 else (3 - x, z)


def column_pairs(step):
    pairs = []
    for i in range(NI):
        for y in range(4):
            for c in range(2):
                pairs.append((i * 8 + y * 2 + c, i * 8 + (y + step) % 4 * 2 + c))
    return pairs


def column(v, step):
    return lax.ppermute(v, BOTH, column_pairs(step))


def ring(v, step):
    return lax.ppermute(v, BOTH, pairs_of(ring_move(step)))


def relayed(prev, following):
    half = ROWS // 2
    return [ring(prev[:half], 1), ring(following[half:], -1)]


def pair(v):
    return lax.ppermute(v, BOTH, pairs_of(pair_move))


def partner(v):
    return lax.ppermute(v, BOTH, pairs_of(partner_move))


def plan_kernel(top_ref, probes_ref, home_ref, y_ref, emb_ref, wg_ref, wu_ref, wo_ref, msg_ref, src_ref, piece_ref, sems):
    part = pl.multiple_of(y_ref[0, 0] * 512, 512)
    cuts = [
        (wg_ref.at[pl.ds(part, 512)], piece_ref.at[pl.ds(0, 512)]),
        (wu_ref.at[pl.ds(part, 512)], piece_ref.at[pl.ds(512, 512)]),
        (wo_ref.at[:, pl.ds(part, FS)], piece_ref.at[pl.ds(1024, FS)]),
        (wo_ref.at[:, pl.ds(pl.multiple_of(part + FS, FS), FS)], piece_ref.at[pl.ds(1024 + FS, FS)]),
    ]
    cuts = [pltpu.make_async_copy(src, dst, sems.at[i]) for i, (src, dst) in enumerate(cuts)]
    for copy in cuts:
        copy.start()
    shape = (NI, 8, 128)
    owner_id = lax.broadcasted_iota(I32, shape, 0)
    lane_id = lax.broadcasted_iota(I32, shape, 2)
    row_id = lax.broadcasted_iota(I32, shape, 1)
    vec = jnp.where(lane_id >= 8, 64, 0)
    owners = []
    for k in range(TOPK):
        loc = home_ref[top_ref[0, k]]
        owner = loc // PASS_DEV
        rank = jnp.int32(0)
        for earlier in owners:
            rank = rank + jnp.where(earlier == owner, 1, 0)
        owners.append(owner)
        src_ref[0, k] = owner * CAP + rank
        vec = jnp.where((owner_id == owner) & (lane_id == rank), loc % PASS_DEV, vec)
    for k in range(NPROBE):
        c = probes_ref[0, k]
        vec = jnp.where((owner_id == c // CLUS_DEV) & (lane_id == 8 + k), c % CLUS_DEV, vec)
    emb = jnp.zeros(shape, F32)
    for c in range(6):
        part_c = emb_ref[:, c * 128 : (c + 1) * 128].astype(F32)
        emb = jnp.where(row_id == c, jnp.broadcast_to(part_c[None], shape), emb)
    msg_ref[...] = jnp.where(row_id == 6, vec.astype(F32), emb).astype(BF16)
    for copy in cuts:
        copy.wait()


def make_plan(top, probes, home, y, emb, w_gate, w_up, w_out):
    any_ = pl.BlockSpec(memory_space=pl.ANY)
    smem = pl.BlockSpec(memory_space=pltpu.SMEM)
    vmem = pl.BlockSpec(memory_space=pltpu.VMEM)
    return pl.pallas_call(
        plan_kernel,
        out_shape=(
            jax.ShapeDtypeStruct((NI, 8, 128), BF16),
            jax.ShapeDtypeStruct((1, TOPK), I32),
            jax.ShapeDtypeStruct((1536, FS), BF16),
        ),
        in_specs=[smem, smem, smem, smem, vmem, any_, any_, any_],
        out_specs=(vmem, smem, vmem),
        scratch_shapes=[pltpu.SemaphoreType.DMA((4,))],
        compiler_params=pltpu.CompilerParams(vmem_limit_bytes=60 * 1024 * 1024),
        name="plan",
    )(top, probes, home, y, emb, w_gate, w_up, w_out)


def ask_kernel(passed, asked_ref, *refs):
    slot_ref = refs[-1 - passed]
    slot_ref[...] = asked_ref[:, 6, :].astype(F32).astype(I32)


def read_asked(asked, passed, after):
    any_ = pl.BlockSpec(memory_space=pl.ANY)
    vmem = pl.BlockSpec(memory_space=pltpu.VMEM)
    return pl.pallas_call(
        functools.partial(ask_kernel, len(passed)),
        out_shape=(
            jax.ShapeDtypeStruct((NI, 128), I32),
            *(jax.ShapeDtypeStruct(v.shape, v.dtype) for v in passed),
        ),
        in_specs=[vmem] + [any_] * (len(passed) + len(after)),
        out_specs=(vmem, *(any_ for _ in passed)),
        input_output_aliases={1 + i: 1 + i for i in range(len(passed))},
        compiler_params=pltpu.CompilerParams(vmem_limit_bytes=48 * 1024 * 1024),
        name="ask",
    )(asked, *passed, *after)


def send_kernel(*refs):
    pass


def send_after(value, *after):
    any_ = pl.BlockSpec(memory_space=pl.ANY)
    return pl.pallas_call(
        send_kernel,
        out_shape=jax.ShapeDtypeStruct(value.shape, value.dtype),
        in_specs=[any_] * (1 + len(after)),
        out_specs=any_,
        input_output_aliases={0: 0},
        compiler_params=pltpu.CompilerParams(vmem_limit_bytes=60 * 1024 * 1024),
        name="send",
    )(value, *after)


def pick_kernel(slot_ref, states_ref, *refs):
    out_ref, sems = refs[(len(refs) - 2) // 2], refs[-1]
    copies = []
    for i in range(NI * CAP):
        row = slot_ref[i // CAP, i % CAP]
        copy = pltpu.make_async_copy(states_ref.at[row], out_ref.at[i], sems.at[i])
        copy.start()
        copies.append(copy)
    for copy in copies:
        copy.wait()


def pick_slots(slots, states, *passed):
    any_ = pl.BlockSpec(memory_space=pl.ANY)
    return pl.pallas_call(
        pick_kernel,
        out_shape=(
            jax.ShapeDtypeStruct((NI * CAP, LP, D), BF16),
            *(jax.ShapeDtypeStruct(v.shape, v.dtype) for v in passed),
        ),
        in_specs=[pl.BlockSpec(memory_space=pltpu.SMEM), any_] + [any_] * len(passed),
        out_specs=(pl.BlockSpec(memory_space=pltpu.VMEM), *(any_ for _ in passed)),
        input_output_aliases={2 + i: 1 + i for i in range(len(passed))},
        scratch_shapes=[pltpu.SemaphoreType.DMA((NI * CAP,))],
        compiler_params=pltpu.CompilerParams(vmem_limit_bytes=57 * 1024 * 1024),
        cost_estimate=pl.CostEstimate(flops=0, bytes_accessed=2 * NI * CAP * LP * D * 2, transcendentals=0),
        name="pick",
    )(slots, states, *passed)


def norm_kernel(src_ref, recv_ref, state_ref, gain_ref, *refs):
    out_ref, buf, sems = refs[-3:]
    copies = []
    for k in range(TOPK):
        copy = pltpu.make_async_copy(recv_ref.at[src_ref[0, k]], buf.at[k], sems.at[k])
        copy.start()
        copies.append(copy)
    state = state_ref[...].astype(F32)
    gain = gain_ref[...]
    for k in range(TOPK // 2):
        copies[2 * k].wait()
        copies[2 * k + 1].wait()
        x = buf[2 * k : 2 * k + 2].astype(F32).reshape(2 * LP, D) + state
        inv = lax.rsqrt(jnp.mean(x * x, axis=-1, keepdims=True) + 1e-06)
        out_ref[2 * LP * k : 2 * LP * (k + 1), :] = (x * inv * gain).astype(BF16)


def norm_rows(src, recv, state, gain, *after):
    vmem = pl.BlockSpec(memory_space=pltpu.VMEM)
    return pl.pallas_call(
        norm_kernel,
        out_shape=jax.ShapeDtypeStruct((ROWS, D), BF16),
        in_specs=[
            pl.BlockSpec(memory_space=pltpu.SMEM),
            pl.BlockSpec(memory_space=pl.ANY),
            vmem,
            vmem,
            *(pl.BlockSpec(memory_space=pl.ANY) for _ in after),
        ],
        out_specs=vmem,
        scratch_shapes=[pltpu.VMEM((TOPK, LP, D), BF16), pltpu.SemaphoreType.DMA((TOPK,))],
        compiler_params=pltpu.CompilerParams(vmem_limit_bytes=57 * 1024 * 1024),
        name="norm",
    )(src, recv, state, gain, *after)


NT = (((1,), (1,)), ((), ()))


def ready_kernel(n_a, n_b, *refs):
    y = refs[0][0, 0]
    blocks = n_a + n_b
    d_in = refs[1 : 1 + blocks]
    wg_in, wu_in, wo_in = refs[1 + blocks : 4 + blocks]
    wp_in = refs[4 + blocks : 8 + blocks]
    wg, wu, da, db, pa, pb, wo, sems = refs[8 + blocks :]
    count = [0]

    def start(src, dst):
        copy = pltpu.make_async_copy(src, dst, sems.at[count[0]])
        count[0] += 1
        copy.start()
        return copy

    parts = [pl.multiple_of((y + j) % 4 * 512, 512) for j in range(4)]
    first = [start(wo_in, wo.at[pl.ds(0, FS)])]
    for j in range(4):
        for h in range(2):
            cols = pl.ds(pl.multiple_of(parts[j] + h * FS, FS), FS)
            first.append(start(wp_in[j].at[pl.ds(1024 + h * FS, FS)], wo.at[pl.ds(FS, FS), cols]))
    at = 0
    for ref in d_in[:n_a]:
        first.append(start(ref, da.at[pl.ds(at, ref.shape[0])]))
        at += ref.shape[0]
    second, at = [], 0
    for ref in d_in[n_a:]:
        second.append(start(ref, db.at[pl.ds(at, ref.shape[0])]))
        at += ref.shape[0]
    third = [start(wg_in, wg.at[:, pl.ds(0, FS)]), start(wu_in, wu.at[:, pl.ds(0, FS)])]
    for j in range(4):
        rows = pl.ds(parts[j], 512)
        third.append(start(wp_in[j].at[pl.ds(0, 512)], wg.at[rows, pl.ds(FS, FS)]))
        third.append(start(wp_in[j].at[pl.ds(512, 512)], wu.at[rows, pl.ds(FS, FS)]))
    for copy in first:
        copy.wait()
    pa[...] = lax.dot_general(da[...], wo[...], NT, preferred_element_type=F32)
    for copy in second:
        copy.wait()
    pb[...] = lax.dot_general(db[...], wo[...], NT, preferred_element_type=F32)
    for copy in third:
        copy.wait()


def make_ready(y, d_a, d_b, weights):
    any_ = pl.BlockSpec(memory_space=pl.ANY)
    vmem = pl.BlockSpec(memory_space=pltpu.VMEM)
    rows = [sum(v.shape[0] for v in d_a), sum(v.shape[0] for v in d_b)]
    out_shape = (
        jax.ShapeDtypeStruct((D, 2 * FS), BF16),
        jax.ShapeDtypeStruct((D, 2 * FS), BF16),
        jax.ShapeDtypeStruct((rows[0], D), BF16),
        jax.ShapeDtypeStruct((rows[1], D), BF16),
        jax.ShapeDtypeStruct((rows[0], 2 * FS), F32),
        jax.ShapeDtypeStruct((rows[1], 2 * FS), F32),
    )
    args = [y, *d_a, *d_b, *weights]
    return pl.pallas_call(
        functools.partial(ready_kernel, len(d_a), len(d_b)),
        out_shape=out_shape,
        in_specs=[pl.BlockSpec(memory_space=pltpu.SMEM)] + [any_] * (len(args) - 1),
        out_specs=tuple(vmem for _ in out_shape),
        scratch_shapes=[pltpu.VMEM((2 * FS, D), BF16), pltpu.SemaphoreType.DMA((19 + len(d_a) + len(d_b),))],
        compiler_params=pltpu.CompilerParams(vmem_limit_bytes=READY_VMEM * 1024 * 1024),
        cost_estimate=pl.CostEstimate(flops=1000, bytes_accessed=1000, transcendentals=0),
        name="ready",
    )(*args)


def layer_kernel(blocks, tile, last, *refs):
    n_in = refs[:blocks]
    wg, wu, dbuf, pre = refs[blocks : blocks + 4]
    rest = refs[blocks + 4 :]
    if last:
        acc_in, gacc_ref, gain_ref, own_out, par_out, gout_ref = rest[:6]
        rest = rest[6:]
    else:
        acc_out, gout_ref = rest[:2]
        rest = rest[2:]
    nbuf, gate_buf, act, dgate, dup, acc, par, sems, out_sems = rest

    copies = []
    for b in range(blocks):
        copies.append(pltpu.make_async_copy(n_in[b], nbuf.at[pl.ds(b * ROWS, ROWS)], sems.at[b]))
        copies[-1].start()
    if last:
        acc_copy = pltpu.make_async_copy(acc_in, acc, sems.at[blocks])
        acc_copy.start()
    tiles = [slice(t * tile, (t + 1) * tile) for t in range(blocks * ROWS // tile)]
    for copy in copies:
        copy.wait()
    for rows in tiles:
        gate_buf[rows, :] = jnp.dot(nbuf[rows, :], wg[...], preferred_element_type=F32)
    for rows in tiles:
        up = jnp.dot(nbuf[rows, :], wu[...], preferred_element_type=F32)
        gate = gate_buf[rows, :]
        d_act = pre[rows, :]
        inner = GELU_C * (gate + 0.044715 * gate * gate * gate)
        th = jnp.tanh(inner)
        half = 0.5 * (1.0 + th)
        gelu = gate * half
        slope = half + 0.5 * gate * (1.0 - th * th) * GELU_C * (1.0 + 3.0 * 0.044715 * gate * gate)
        act[rows, :] = (gelu * up).astype(BF16)
        dgate[rows, :] = (d_act * up * slope).astype(BF16)
        dup[rows, :] = (d_act * gelu).astype(BF16)
    if last:
        acc_copy.wait()
    act_t = act[...].T
    leaving = []
    for r in range(NR):
        cols = slice(r * FS, (r + 1) * FS)
        part = jnp.dot(act_t, dbuf[:, cols], preferred_element_type=F32)
        if last:
            part = part + acc[r]
            acc[r, :FS] = part[:FS]
            par[r] = part[FS:].astype(BF16)
            leaving.append(pltpu.make_async_copy(acc.at[r, pl.ds(0, FS)], own_out.at[r], out_sems.at[2 * r]))
            leaving.append(pltpu.make_async_copy(par.at[r], par_out.at[r], out_sems.at[2 * r + 1]))
            leaving[-2].start()
            leaving[-1].start()
        else:
            acc[r] = part
            leaving.append(pltpu.make_async_copy(acc.at[r], acc_out.at[r], out_sems.at[r]))
            leaving[-1].start()

    for j in range(4):
        cols = slice(j * 512, (j + 1) * 512)
        dn = lax.dot_general(dgate[...], wg[cols, :], NT, preferred_element_type=F32)
        dn = dn + lax.dot_general(dup[...], wu[cols, :], NT, preferred_element_type=F32)
        part = jnp.sum(dn * nbuf[:, cols].astype(F32), axis=0, keepdims=True)
        if last:
            part = (part + gacc_ref[:, cols]) / gain_ref[:, cols]
        gout_ref[:, cols] = part
    for copy in leaving:
        copy.wait()


def layer(n_blocks, ready, tile, carried=None):
    blocks = len(n_blocks)
    rows = blocks * ROWS
    last = carried is not None
    any_ = pl.BlockSpec(memory_space=pl.ANY)
    vmem = pl.BlockSpec(memory_space=pltpu.VMEM)
    args = [*n_blocks, *ready]
    in_specs = [any_] * blocks + [vmem] * len(ready)
    if last:
        args += list(carried)
        in_specs += [any_, vmem, vmem]
        out_shape = (
            jax.ShapeDtypeStruct((NR, FS, FS), F32),
            jax.ShapeDtypeStruct((NR, FS, FS), BF16),
            jax.ShapeDtypeStruct((1, D), F32),
        )
    else:
        out_shape = (
            jax.ShapeDtypeStruct((NR, 2 * FS, FS), F32),
            jax.ShapeDtypeStruct((1, D), F32),
        )
    return pl.pallas_call(
        functools.partial(layer_kernel, blocks, tile, last),
        out_shape=out_shape,
        in_specs=in_specs,
        out_specs=(*(any_ for _ in out_shape[1:]), vmem),
        scratch_shapes=[
            pltpu.VMEM((rows, D), BF16),
            pltpu.VMEM((rows, 2 * FS), F32),
            pltpu.VMEM((rows, 2 * FS), BF16),
            pltpu.VMEM((rows, 2 * FS), BF16),
            pltpu.VMEM((rows, 2 * FS), BF16),
            pltpu.VMEM((NR, 2 * FS, FS), F32),
            pltpu.VMEM((NR, FS, FS), BF16),
            pltpu.SemaphoreType.DMA((blocks + 1,)),
            pltpu.SemaphoreType.DMA((2 * NR,)),
        ],
        compiler_params=pltpu.CompilerParams(vmem_limit_bytes=LAYER_VMEM * 1024 * 1024),
        cost_estimate=pl.CostEstimate(
            flops=10 * rows * D * 2 * FS, bytes_accessed=4 * rows * D, transcendentals=rows * 512
        ),
        name="layer_last" if last else "layer_first",
    )(*args)


def merge_kernel(own_ref, other_ref, rows_ref, out_ref):
    for r in range(NR):
        out_ref[r, :FS] = (own_ref[r] + other_ref[r].astype(F32)).astype(BF16)
        out_ref[r, FS:] = rows_ref[r]


def merge(own, other, rows):
    vmem = pl.BlockSpec(memory_space=pltpu.VMEM)
    return pl.pallas_call(
        merge_kernel,
        out_shape=jax.ShapeDtypeStruct((NR, FS + 16, FS), BF16),
        in_specs=[vmem] * 3,
        out_specs=vmem,
        compiler_params=pltpu.CompilerParams(vmem_limit_bytes=16 * 1024 * 1024),
        name="merge",
    )(own, other, rows)


def shards(
    question_emb,
    probes,
    codes,
    code_scale,
    question_state,
    top_passages,
    soft_weight,
    passage_home,
    passage_states,
    norm_gain,
    w_gate,
    w_up,
    w_out,
    cotangent,
):
    dy0 = (soft_weight[:, :, None, None] * cotangent.astype(F32)).astype(BF16).reshape(ROWS, D)
    dyp = pair(dy0)
    dy_m = ring(dy0, 1)
    dy_p = ring(dy0, -1)
    y_row = (lax.axis_index("reader") // 2).astype(I32).reshape(1, 1)

    msg, src, piece = make_plan(
        top_passages, probes, passage_home, y_row, question_emb, w_gate, w_up, w_out
    )
    piece = partner(piece)
    asked = lax.all_to_all(msg, "index", 0, 0, tiled=True)
    slots, piece, dyp = read_asked(asked, (piece, dyp), (dy_m, dy_p))
    weights = (w_gate, w_up, w_out, piece, column(piece, -1), column(piece, 2), column(piece, 1))
    dyp_m = ring(dyp, 1)
    dyp_p = ring(dyp, -1)
    (blocks,) = pick_slots(slots, passage_states)
    blocks = send_after(blocks, dyp_m, dyp_p)
    recv = lax.all_to_all(blocks, "index", 0, 0, tiled=True)
    dy_a = [dy0, dy_m, dy_p, ring(dy0, 2), dyp]
    dy_b = [dyp_m, dyp_p, ring(dyp, 2)]
    group_emb = asked[:, :6, :].reshape(NI, 768)
    every_score = (
        jnp.einsum("qe,cse->qcs", group_emb, codes, preferred_element_type=F32) * code_scale[None]
    )
    local = asked[:, 6, 8 : 8 + NPROBE].astype(I32)
    hot = (local[:, :, None] == jnp.arange(CLUS_DEV, dtype=I32)[None, None, :]).astype(F32)
    picked = jnp.einsum("qpc,qcs->qps", hot, every_score, precision=lax.Precision.HIGHEST)
    picked = picked.astype(BF16)

    gain_row = norm_gain.reshape(1, D)
    n0 = norm_rows(src, recv, question_state, gain_row, picked)
    np_ = pair(n0)
    n_a = [n0, ring(n0, 1), ring(n0, -1), ring(n0, 2), np_]
    n_b = [ring(np_, 1), ring(np_, -1), ring(np_, 2)]

    wg2, wu2, d_rows_a, d_rows_b, d_act_a, d_act_b = make_ready(y_row, dy_a, dy_b, weights)
    acc_a, gain_a = layer(n_a, (wg2, wu2, d_rows_a, d_act_a), FIRST_TILE)
    own, par, gain_part = layer(
        n_b, (wg2, wu2, d_rows_b, d_act_b), LAST_TILE, (acc_a, gain_a, gain_row)
    )

    from_partner = partner(par)
    gain_own = gain_part.reshape(NI, 1, 128)
    gain_hi = gain_own.astype(BF16)
    gain_lo = (gain_own - gain_hi.astype(F32)).astype(BF16)
    tail = jnp.concatenate([picked, gain_hi, gain_lo, jnp.zeros((NI, 6, 128), BF16)], axis=1)
    tail = lax.all_to_all(tail, "index", 0, 0, tiled=True)
    tail = jnp.sum(tail.astype(F32), axis=0)
    probe_scores = tail[None, :NPROBE]
    gain128 = (tail[NPROBE] + tail[NPROBE + 1]).reshape(NR, 1, 16)
    hi = gain128.astype(BF16)
    lo = (gain128 - hi.astype(F32)).astype(BF16)
    gain_rows = jnp.pad(jnp.concatenate([hi, lo], axis=2), ((0, 0), (0, 15), (0, FS - 32)))
    out = lax.all_to_all(merge(own, from_partner, gain_rows), "reader", 0, 0, tiled=True)
    grad_out = jnp.sum(out[:, :FS].astype(F32), axis=0)
    gain_out = jnp.sum(out[:, FS, :32].astype(F32), axis=0)
    grad_gain = gain_out[:16] + gain_out[16:]
    return probe_scores, grad_out, grad_gain


def solution(mesh):
    return jax.shard_map(
        shards,
        mesh=mesh,
        in_specs=(
            P(("index", "reader"), None),
            P(("index", "reader"), None),
            P("index", None, None),
            P("index", None),
            P(("index", "reader"), None),
            P(("index", "reader"), None),
            P(("index", "reader"), None),
            P(),
            P("index", None, None),
            P(),
            P(None, "index"),
            P(None, "index"),
            P("index", None),
            P(("index", "reader"), None, None, None),
        ),
        out_specs=(
            P(("index", "reader"), None, None),
            P("index", "reader"),
            P(("index", "reader")),
        ),
        check_vma=False,
    )
```

```python
import functools
import math

import jax
import jax.numpy as jnp
from jax import lax
from jax.experimental import pallas as pl
from jax.experimental.pallas import tpu as pltpu
from jax.sharding import PartitionSpec as P

BF16 = jnp.bfloat16
F32 = jnp.float32
I32 = jnp.int32

CAP = 3
FIRST_TILE = 400
LAST_TILE = 480
READY_VMEM = 20
LAYER_VMEM = 26
NI = 16
NR = 8
TOPK = 20
NPROBE = 32
LP = 8
D = 2048
FS = 256
ROWS = TOPK * LP
PASS_DEV = 256
CLUS_DEV = 32
GELU_C = math.sqrt(2.0 / math.pi)
BOTH = ("index", "reader")


def pairs_of(move):
    pairs = []
    for x in range(4):
        for z in range(4):
            for y in range(4):
                for c in range(2):
                    tx, tz = move(x, z, c)
                    pairs.append(((x * 4 + z) * 8 + y * 2 + c, (tx * 4 + tz) * 8 + y * 2 + c))
    return pairs


def ring_move(step):
    return lambda x, z, c: ((x + step) % 4, z) if c == 0 else (x, (z + step) % 4)


def pair_move(x, z, c):
    return (x, z ^ 1) if c == 0 else (x ^ 1, z)


def partner_move(x, z, c):
    return (x, 3 - z) if c == 0 else (3 - x, z)


def column_pairs(step):
    pairs = []
    for i in range(NI):
        for y in range(4):
            for c in range(2):
                pairs.append((i * 8 + y * 2 + c, i * 8 + (y + step) % 4 * 2 + c))
    return pairs


def column(v, step):
    return lax.ppermute(v, BOTH, column_pairs(step))


def ring(v, step):
    return lax.ppermute(v, BOTH, pairs_of(ring_move(step)))


def relayed(prev, following):
    half = ROWS // 2
    return [ring(prev[:half], 1), ring(following[half:], -1)]


def pair(v):
    return lax.ppermute(v, BOTH, pairs_of(pair_move))


def partner(v):
    return lax.ppermute(v, BOTH, pairs_of(partner_move))


def plan_kernel(top_ref, probes_ref, home_ref, y_ref, emb_ref, wg_ref, wu_ref, wo_ref, msg_ref, src_ref, piece_ref, sems):
    part = pl.multiple_of(y_ref[0, 0] * 512, 512)
    cuts = [
        (wg_ref.at[pl.ds(part, 512)], piece_ref.at[pl.ds(0, 512)]),
        (wu_ref.at[pl.ds(part, 512)], piece_ref.at[pl.ds(512, 512)]),
        (wo_ref.at[:, pl.ds(part, FS)], piece_ref.at[pl.ds(1024, FS)]),
        (wo_ref.at[:, pl.ds(pl.multiple_of(part + FS, FS), FS)], piece_ref.at[pl.ds(1024 + FS, FS)]),
    ]
    cuts = [pltpu.make_async_copy(src, dst, sems.at[i]) for i, (src, dst) in enumerate(cuts)]
    for copy in cuts:
        copy.start()
    shape = (NI, 8, 128)
    owner_id = lax.broadcasted_iota(I32, shape, 0)
    lane_id = lax.broadcasted_iota(I32, shape, 2)
    row_id = lax.broadcasted_iota(I32, shape, 1)
    vec = jnp.where(lane_id >= 8, 64, 0)
    owners = []
    for k in range(TOPK):
        loc = home_ref[top_ref[0, k]]
        owner = loc // PASS_DEV
        rank = jnp.int32(0)
        for earlier in owners:
            rank = rank + jnp.where(earlier == owner, 1, 0)
        owners.append(owner)
        src_ref[0, k] = owner * CAP + rank
        vec = jnp.where((owner_id == owner) & (lane_id == rank), loc % PASS_DEV, vec)
    for k in range(NPROBE):
        c = probes_ref[0, k]
        vec = jnp.where((owner_id == c // CLUS_DEV) & (lane_id == 8 + k), c % CLUS_DEV, vec)
    emb = jnp.zeros(shape, F32)
    for c in range(6):
        part_c = emb_ref[:, c * 128 : (c + 1) * 128].astype(F32)
        emb = jnp.where(row_id == c, jnp.broadcast_to(part_c[None], shape), emb)
    msg_ref[...] = jnp.where(row_id == 6, vec.astype(F32), emb).astype(BF16)
    for copy in cuts:
        copy.wait()


def make_plan(top, probes, home, y, emb, w_gate, w_up, w_out):
    any_ = pl.BlockSpec(memory_space=pl.ANY)
    smem = pl.BlockSpec(memory_space=pltpu.SMEM)
    vmem = pl.BlockSpec(memory_space=pltpu.VMEM)
    return pl.pallas_call(
        plan_kernel,
        out_shape=(
            jax.ShapeDtypeStruct((NI, 8, 128), BF16),
            jax.ShapeDtypeStruct((1, TOPK), I32),
            jax.ShapeDtypeStruct((1536, FS), BF16),
        ),
        in_specs=[smem, smem, smem, smem, vmem, any_, any_, any_],
        out_specs=(vmem, smem, vmem),
        scratch_shapes=[pltpu.SemaphoreType.DMA((4,))],
        compiler_params=pltpu.CompilerParams(vmem_limit_bytes=60 * 1024 * 1024),
        name="plan",
    )(top, probes, home, y, emb, w_gate, w_up, w_out)


def ask_kernel(passed, asked_ref, *refs):
    slot_ref = refs[-1 - passed]
    slot_ref[...] = asked_ref[:, 6, :].astype(F32).astype(I32)


def read_asked(asked, passed, after):
    any_ = pl.BlockSpec(memory_space=pl.ANY)
    vmem = pl.BlockSpec(memory_space=pltpu.VMEM)
    return pl.pallas_call(
        functools.partial(ask_kernel, len(passed)),
        out_shape=(
            jax.ShapeDtypeStruct((NI, 128), I32),
            *(jax.ShapeDtypeStruct(v.shape, v.dtype) for v in passed),
        ),
        in_specs=[vmem] + [any_] * (len(passed) + len(after)),
        out_specs=(vmem, *(any_ for _ in passed)),
        input_output_aliases={1 + i: 1 + i for i in range(len(passed))},
        compiler_params=pltpu.CompilerParams(vmem_limit_bytes=48 * 1024 * 1024),
        name="ask",
    )(asked, *passed, *after)


def send_kernel(*refs):
    pass


def send_after(value, *after):
    any_ = pl.BlockSpec(memory_space=pl.ANY)
    return pl.pallas_call(
        send_kernel,
        out_shape=jax.ShapeDtypeStruct(value.shape, value.dtype),
        in_specs=[any_] * (1 + len(after)),
        out_specs=any_,
        input_output_aliases={0: 0},
        compiler_params=pltpu.CompilerParams(vmem_limit_bytes=60 * 1024 * 1024),
        name="send",
    )(value, *after)


def pick_kernel(slot_ref, states_ref, *refs):
    out_ref, sems = refs[(len(refs) - 2) // 2], refs[-1]
    copies = []
    for i in range(NI * CAP):
        row = slot_ref[i // CAP, i % CAP]
        copy = pltpu.make_async_copy(states_ref.at[row], out_ref.at[i], sems.at[i])
        copy.start()
        copies.append(copy)
    for copy in copies:
        copy.wait()


def pick_slots(slots, states, *passed):
    any_ = pl.BlockSpec(memory_space=pl.ANY)
    return pl.pallas_call(
        pick_kernel,
        out_shape=(
            jax.ShapeDtypeStruct((NI * CAP, LP, D), BF16),
            *(jax.ShapeDtypeStruct(v.shape, v.dtype) for v in passed),
        ),
        in_specs=[pl.BlockSpec(memory_space=pltpu.SMEM), any_] + [any_] * len(passed),
        out_specs=(pl.BlockSpec(memory_space=pltpu.VMEM), *(any_ for _ in passed)),
        input_output_aliases={2 + i: 1 + i for i in range(len(passed))},
        scratch_shapes=[pltpu.SemaphoreType.DMA((NI * CAP,))],
        compiler_params=pltpu.CompilerParams(vmem_limit_bytes=57 * 1024 * 1024),
        cost_estimate=pl.CostEstimate(flops=0, bytes_accessed=2 * NI * CAP * LP * D * 2, transcendentals=0),
        name="pick",
    )(slots, states, *passed)


def norm_kernel(src_ref, recv_ref, state_ref, gain_ref, *refs):
    out_ref, buf, sems = refs[-3:]
    copies = []
    for k in range(TOPK):
        copy = pltpu.make_async_copy(recv_ref.at[src_ref[0, k]], buf.at[k], sems.at[k])
        copy.start()
        copies.append(copy)
    state = state_ref[...].astype(F32)
    gain = gain_ref[...]
    for k in range(TOPK // 2):
        copies[2 * k].wait()
        copies[2 * k + 1].wait()
        x = buf[2 * k : 2 * k + 2].astype(F32).reshape(2 * LP, D) + state
        inv = lax.rsqrt(jnp.mean(x * x, axis=-1, keepdims=True) + 1e-06)
        out_ref[2 * LP * k : 2 * LP * (k + 1), :] = (x * inv * gain).astype(BF16)


def norm_rows(src, recv, state, gain, *after):
    vmem = pl.BlockSpec(memory_space=pltpu.VMEM)
    return pl.pallas_call(
        norm_kernel,
        out_shape=jax.ShapeDtypeStruct((ROWS, D), BF16),
        in_specs=[
            pl.BlockSpec(memory_space=pltpu.SMEM),
            pl.BlockSpec(memory_space=pl.ANY),
            vmem,
            vmem,
            *(pl.BlockSpec(memory_space=pl.ANY) for _ in after),
        ],
        out_specs=vmem,
        scratch_shapes=[pltpu.VMEM((TOPK, LP, D), BF16), pltpu.SemaphoreType.DMA((TOPK,))],
        compiler_params=pltpu.CompilerParams(vmem_limit_bytes=57 * 1024 * 1024),
        name="norm",
    )(src, recv, state, gain, *after)


NT = (((1,), (1,)), ((), ()))


def ready_kernel(n_a, n_b, *refs):
    y = refs[0][0, 0]
    blocks = n_a + n_b
    d_in = refs[1 : 1 + blocks]
    wg_in, wu_in, wo_in = refs[1 + blocks : 4 + blocks]
    wp_in = refs[4 + blocks : 8 + blocks]
    wg, wu, da, db, pa, pb, wo, sems = refs[8 + blocks :]
    count = [0]

    def start(src, dst):
        copy = pltpu.make_async_copy(src, dst, sems.at[count[0]])
        count[0] += 1
        copy.start()
        return copy

    parts = [pl.multiple_of((y + j) % 4 * 512, 512) for j in range(4)]
    first = [start(wo_in, wo.at[pl.ds(0, FS)])]
    for j in range(4):
        for h in range(2):
            cols = pl.ds(pl.multiple_of(parts[j] + h * FS, FS), FS)
            first.append(start(wp_in[j].at[pl.ds(1024 + h * FS, FS)], wo.at[pl.ds(FS, FS), cols]))
    at = 0
    for ref in d_in[:n_a]:
        first.append(start(ref, da.at[pl.ds(at, ref.shape[0])]))
        at += ref.shape[0]
    second, at = [], 0
    for ref in d_in[n_a:]:
        second.append(start(ref, db.at[pl.ds(at, ref.shape[0])]))
        at += ref.shape[0]
    third = [start(wg_in, wg.at[:, pl.ds(0, FS)]), start(wu_in, wu.at[:, pl.ds(0, FS)])]
    for j in range(4):
        rows = pl.ds(parts[j], 512)
        third.append(start(wp_in[j].at[pl.ds(0, 512)], wg.at[rows, pl.ds(FS, FS)]))
        third.append(start(wp_in[j].at[pl.ds(512, 512)], wu.at[rows, pl.ds(FS, FS)]))
    for copy in first:
        copy.wait()
    pa[...] = lax.dot_general(da[...], wo[...], NT, preferred_element_type=F32)
    for copy in second:
        copy.wait()
    pb[...] = lax.dot_general(db[...], wo[...], NT, preferred_element_type=F32)
    for copy in third:
        copy.wait()


def make_ready(y, d_a, d_b, weights):
    any_ = pl.BlockSpec(memory_space=pl.ANY)
    vmem = pl.BlockSpec(memory_space=pltpu.VMEM)
    rows = [sum(v.shape[0] for v in d_a), sum(v.shape[0] for v in d_b)]
    out_shape = (
        jax.ShapeDtypeStruct((D, 2 * FS), BF16),
        jax.ShapeDtypeStruct((D, 2 * FS), BF16),
        jax.ShapeDtypeStruct((rows[0], D), BF16),
        jax.ShapeDtypeStruct((rows[1], D), BF16),
        jax.ShapeDtypeStruct((rows[0], 2 * FS), F32),
        jax.ShapeDtypeStruct((rows[1], 2 * FS), F32),
    )
    args = [y, *d_a, *d_b, *weights]
    return pl.pallas_call(
        functools.partial(ready_kernel, len(d_a), len(d_b)),
        out_shape=out_shape,
        in_specs=[pl.BlockSpec(memory_space=pltpu.SMEM)] + [any_] * (len(args) - 1),
        out_specs=tuple(vmem for _ in out_shape),
        scratch_shapes=[pltpu.VMEM((2 * FS, D), BF16), pltpu.SemaphoreType.DMA((19 + len(d_a) + len(d_b),))],
        compiler_params=pltpu.CompilerParams(vmem_limit_bytes=READY_VMEM * 1024 * 1024),
        cost_estimate=pl.CostEstimate(flops=1000, bytes_accessed=1000, transcendentals=0),
        name="ready",
    )(*args)


def layer_kernel(blocks, tile, last, *refs):
    n_in = refs[:blocks]
    wg, wu, dbuf, pre = refs[blocks : blocks + 4]
    rest = refs[blocks + 4 :]
    if last:
        acc_in, gacc_ref, gain_ref, own_out, par_out, gout_ref = rest[:6]
        rest = rest[6:]
    else:
        acc_out, gout_ref = rest[:2]
        rest = rest[2:]
    nbuf, gate_buf, act, dgate, dup, acc, par, sems, out_sems = rest

    copies = []
    for b in range(blocks):
        copies.append(pltpu.make_async_copy(n_in[b], nbuf.at[pl.ds(b * ROWS, ROWS)], sems.at[b]))
        copies[-1].start()
    if last:
        acc_copy = pltpu.make_async_copy(acc_in, acc, sems.at[blocks])
        acc_copy.start()
    tiles = [slice(t * tile, (t + 1) * tile) for t in range(blocks * ROWS // tile)]
    for copy in copies:
        copy.wait()
    for rows in tiles:
        gate_buf[rows, :] = jnp.dot(nbuf[rows, :], wg[...], preferred_element_type=F32)
    for rows in tiles:
        up = jnp.dot(nbuf[rows, :], wu[...], preferred_element_type=F32)
        gate = gate_buf[rows, :]
        d_act = pre[rows, :]
        inner = GELU_C * (gate + 0.044715 * gate * gate * gate)
        th = jnp.tanh(inner)
        half = 0.5 * (1.0 + th)
        gelu = gate * half
        slope = half + 0.5 * gate * (1.0 - th * th) * GELU_C * (1.0 + 3.0 * 0.044715 * gate * gate)
        act[rows, :] = (gelu * up).astype(BF16)
        dgate[rows, :] = (d_act * up * slope).astype(BF16)
        dup[rows, :] = (d_act * gelu).astype(BF16)
    if last:
        acc_copy.wait()
    act_t = act[...].T
    leaving = []
    for r in range(NR):
        cols = slice(r * FS, (r + 1) * FS)
        part = jnp.dot(act_t, dbuf[:, cols], preferred_element_type=F32)
        if last:
            part = part + acc[r]
            acc[r, :FS] = part[:FS]
            par[r] = part[FS:].astype(BF16)
            leaving.append(pltpu.make_async_copy(acc.at[r, pl.ds(0, FS)], own_out.at[r], out_sems.at[2 * r]))
            leaving.append(pltpu.make_async_copy(par.at[r], par_out.at[r], out_sems.at[2 * r + 1]))
            leaving[-2].start()
            leaving[-1].start()
        else:
            acc[r] = part
            leaving.append(pltpu.make_async_copy(acc.at[r], acc_out.at[r], out_sems.at[r]))
            leaving[-1].start()

    for j in range(4):
        cols = slice(j * 512, (j + 1) * 512)
        dn = lax.dot_general(dgate[...], wg[cols, :], NT, preferred_element_type=F32)
        dn = dn + lax.dot_general(dup[...], wu[cols, :], NT, preferred_element_type=F32)
        part = jnp.sum(dn * nbuf[:, cols].astype(F32), axis=0, keepdims=True)
        if last:
            part = (part + gacc_ref[:, cols]) / gain_ref[:, cols]
        gout_ref[:, cols] = part
    for copy in leaving:
        copy.wait()


def layer(n_blocks, ready, tile, carried=None):
    blocks = len(n_blocks)
    rows = blocks * ROWS
    last = carried is not None
    any_ = pl.BlockSpec(memory_space=pl.ANY)
    vmem = pl.BlockSpec(memory_space=pltpu.VMEM)
    args = [*n_blocks, *ready]
    in_specs = [any_] * blocks + [vmem] * len(ready)
    if last:
        args += list(carried)
        in_specs += [any_, vmem, vmem]
        out_shape = (
            jax.ShapeDtypeStruct((NR, FS, FS), F32),
            jax.ShapeDtypeStruct((NR, FS, FS), BF16),
            jax.ShapeDtypeStruct((1, D), F32),
        )
    else:
        out_shape = (
            jax.ShapeDtypeStruct((NR, 2 * FS, FS), F32),
            jax.ShapeDtypeStruct((1, D), F32),
        )
    return pl.pallas_call(
        functools.partial(layer_kernel, blocks, tile, last),
        out_shape=out_shape,
        in_specs=in_specs,
        out_specs=(*(any_ for _ in out_shape[1:]), vmem),
        scratch_shapes=[
            pltpu.VMEM((rows, D), BF16),
            pltpu.VMEM((rows, 2 * FS), F32),
            pltpu.VMEM((rows, 2 * FS), BF16),
            pltpu.VMEM((rows, 2 * FS), BF16),
            pltpu.VMEM((rows, 2 * FS), BF16),
            pltpu.VMEM((NR, 2 * FS, FS), F32),
            pltpu.VMEM((NR, FS, FS), BF16),
            pltpu.SemaphoreType.DMA((blocks + 1,)),
            pltpu.SemaphoreType.DMA((2 * NR,)),
        ],
        compiler_params=pltpu.CompilerParams(vmem_limit_bytes=LAYER_VMEM * 1024 * 1024),
        cost_estimate=pl.CostEstimate(
            flops=10 * rows * D * 2 * FS, bytes_accessed=4 * rows * D, transcendentals=rows * 512
        ),
        name="layer_last" if last else "layer_first",
    )(*args)


def merge_kernel(own_ref, other_ref, rows_ref, out_ref):
    for r in range(NR):
        out_ref[r, :FS] = (own_ref[r] + other_ref[r].astype(F32)).astype(BF16)
        out_ref[r, FS:] = rows_ref[r]


def merge(own, other, rows):
    vmem = pl.BlockSpec(memory_space=pltpu.VMEM)
    return pl.pallas_call(
        merge_kernel,
        out_shape=jax.ShapeDtypeStruct((NR, FS + 16, FS), BF16),
        in_specs=[vmem] * 3,
        out_specs=vmem,
        compiler_params=pltpu.CompilerParams(vmem_limit_bytes=16 * 1024 * 1024),
        name="merge",
    )(own, other, rows)


def shards(
    question_emb,
    probes,
    codes,
    code_scale,
    question_state,
    top_passages,
    soft_weight,
    passage_home,
    passage_states,
    norm_gain,
    w_gate,
    w_up,
    w_out,
    cotangent,
):
    dy0 = (soft_weight[:, :, None, None] * cotangent.astype(F32)).astype(BF16).reshape(ROWS, D)
    dyp = pair(dy0)
    dy_m = ring(dy0, 1)
    dy_p = ring(dy0, -1)
    y_row = (lax.axis_index("reader") // 2).astype(I32).reshape(1, 1)

    msg, src, piece = make_plan(
        top_passages, probes, passage_home, y_row, question_emb, w_gate, w_up, w_out
    )
    piece = partner(piece)
    asked = lax.all_to_all(msg, "index", 0, 0, tiled=True)
    slots, piece = read_asked(asked, (piece,), (dyp, dy_m, dy_p))
    weights = (w_gate, w_up, w_out, piece, column(piece, -1), column(piece, 2), column(piece, 1))
    dyp_m = ring(dyp, 1)
    dyp_p = ring(dyp, -1)
    (blocks,) = pick_slots(slots, passage_states)
    blocks = send_after(blocks, dyp_m, dyp_p)
    recv = lax.all_to_all(blocks, "index", 0, 0, tiled=True)
    dy_a = [dy0, dy_m, dy_p, ring(dy0, 2), dyp]
    dy_b = [dyp_m, dyp_p, ring(dyp, 2)]
    group_emb = asked[:, :6, :].reshape(NI, 768)
    every_score = (
        jnp.einsum("qe,cse->qcs", group_emb, codes, preferred_element_type=F32) * code_scale[None]
    )
    local = asked[:, 6, 8 : 8 + NPROBE].astype(I32)
    hot = (local[:, :, None] == jnp.arange(CLUS_DEV, dtype=I32)[None, None, :]).astype(F32)
    picked = jnp.einsum("qpc,qcs->qps", hot, every_score, precision=lax.Precision.HIGHEST)
    picked = picked.astype(BF16)

    gain_row = norm_gain.reshape(1, D)
    n0 = norm_rows(src, recv, question_state, gain_row, picked)
    np_ = pair(n0)
    n_a = [n0, ring(n0, 1), ring(n0, -1), ring(n0, 2), np_]
    n_b = [ring(np_, 1), ring(np_, -1), ring(np_, 2)]

    wg2, wu2, d_rows_a, d_rows_b, d_act_a, d_act_b = make_ready(y_row, dy_a, dy_b, weights)
    acc_a, gain_a = layer(n_a, (wg2, wu2, d_rows_a, d_act_a), FIRST_TILE)
    own, par, gain_part = layer(
        n_b, (wg2, wu2, d_rows_b, d_act_b), LAST_TILE, (acc_a, gain_a, gain_row)
    )

    from_partner = partner(par)
    gain_own = gain_part.reshape(NI, 1, 128)
    gain_hi = gain_own.astype(BF16)
    gain_lo = (gain_own - gain_hi.astype(F32)).astype(BF16)
    tail = jnp.concatenate([picked, gain_hi, gain_lo, jnp.zeros((NI, 6, 128), BF16)], axis=1)
    tail = lax.all_to_all(tail, "index", 0, 0, tiled=True)
    tail = jnp.sum(tail.astype(F32), axis=0)
    probe_scores = tail[None, :NPROBE]
    gain128 = (tail[NPROBE] + tail[NPROBE + 1]).reshape(NR, 1, 16)
    hi = gain128.astype(BF16)
    lo = (gain128 - hi.astype(F32)).astype(BF16)
    gain_rows = jnp.pad(jnp.concatenate([hi, lo], axis=2), ((0, 0), (0, 15), (0, FS - 32)))
    out = lax.all_to_all(merge(own, from_partner, gain_rows), "reader", 0, 0, tiled=True)
    grad_out = jnp.sum(out[:, :FS].astype(F32), axis=0)
    gain_out = jnp.sum(out[:, FS, :32].astype(F32), axis=0)
    grad_gain = gain_out[:16] + gain_out[16:]
    return probe_scores, grad_out, grad_gain


def solution(mesh):
    return jax.shard_map(
        shards,
        mesh=mesh,
        in_specs=(
            P(("index", "reader"), None),
            P(("index", "reader"), None),
            P("index", None, None),
            P("index", None),
            P(("index", "reader"), None),
            P(("index", "reader"), None),
            P(("index", "reader"), None),
            P(),
            P("index", None, None),
            P(),
            P(None, "index"),
            P(None, "index"),
            P("index", None),
            P(("index", "reader"), None, None, None),
        ),
        out_specs=(
            P(("index", "reader"), None, None),
            P("index", "reader"),
            P(("index", "reader")),
        ),
        check_vma=False,
    )
```
